32 devices in a mesh: energy: 8 (over z, y), rows: 4 (over x, core).
Axes of the slice: x: 2, y: 2, z: 4, core: 2. Of those that a mesh axis runs over, the one named last changes fastest.
Arguments:
- green_window: bfloat16 [2, 2, 16, 4, 9216], P(None, None, 'energy', 'rows'), may hold values from -6 to 6
- screened: bfloat16 [2, 2, 16, 4, 9216], P(None, None, None, 'rows', 'energy'), may hold values from -6 to 6
- retarded: bfloat16 [2, 16, 4, 3, 96, 192], P(None, 'energy', 'rows'), may hold values from -0.375 to 0.375
- energy_order: int32 [16], replicated, may hold values from 0 to 15, each once
- window_start: int32 [4], P('rows'), may hold values from 0 to 96
Outputs:
- density: float32 [2, 2, 16, 4, 192], P(None, None, 'energy', 'rows')
The draws below stay inside these ranges and needn't reach their ends.
Inputs may be any that keep to these rules, and one draw needn't show every extreme that they name: A permutation of the energy indices: slot s holds energy energy_order[s]. Block row i's window covers its orbitals window_start[i] to window_start[i] + 95.
All inputs are finite; a program needn't handle non-finite values.
Results may differ from the reference program's by a relative error of at most 0.0029.
Values may be sent and summed in bfloat16 or wider, within the bound.
No kernel may reach another device: no remote copies, remote signals or barrier semaphores. Data moves between devices by JAX's collectives and lax.ppermute only.
A program may use at most 64 MiB of HBM per device.

```python
import jax
import jax.numpy as jnp
from jax import lax

B = 192
SLAB = 96
NE = 16
NB = 4


def with_ends(values, rng, least, largest):
    shape = values.shape
    spot = [jax.random.randint(jax.random.fold_in(rng, axis), (), 0, shape[axis]) for axis in range(len(shape))]
    values = values.at[tuple(spot)].set(least)
    longest = shape.index(max(shape))
    spot[longest] = (spot[longest] + 1) % shape[longest]
    return values.at[tuple(spot)].set(largest)


def block_levels(rng, extent, pieces, least, top_value):
    level = 1.0
    for axis_at, parts in pieces:
        draws = jax.random.uniform(jax.random.fold_in(jax.random.fold_in(rng, 6), axis_at), (parts,), jnp.float32, least / len(pieces), top_value / len(pieces))
        level = level * jnp.repeat(jnp.exp(draws), extent[axis_at] // parts).reshape((-1,) + (1,) * (len(extent) - 1 - axis_at))
    return level


def bell_draw(key, dims, scale, limit, cuts=(), kind=jnp.bfloat16):
    gain = block_levels(key, dims, cuts, -0.22, 0.18) if cuts else 1.0
    array = jax.random.normal(key, dims, jnp.float32) * scale * gain
    return jnp.minimum(jnp.maximum(array, -limit), limit).astype(kind)


def setup_inputs(seed: int = 0) -> dict:
    keys = jax.random.split(jax.random.key(seed), 6)
    return {
        "green_window": bell_draw(keys[0], (2, 2, NE, NB, SLAB * SLAB), 1.0, 6.0, ((2, 8), (3, 4))),
        "screened": bell_draw(keys[1], (2, 2, NE, NB, SLAB * SLAB), 1.0, 6.0, ((3, 4), (4, 8))),
        "retarded": bell_draw(keys[2], (2, NE, NB, 3, SLAB, B), (3 * SLAB) ** -0.5, 0.375, ((1, 8), (2, 4))),
        "energy_order": jax.random.permutation(keys[3], NE).astype(jnp.int32),
        "window_start": with_ends(jax.random.randint(keys[4], (NB,), 0, B - SLAB + 1), jax.random.fold_in(keys[4], 1), 0, B - SLAB).astype(jnp.int32),
    }


def convolve_row(green_row, screen_row):
    green_complex = lax.complex(green_row[:, 0], green_row[:, 1])
    screen_complex = lax.complex(screen_row[:, 0], screen_row[:, 1])
    times = jnp.fft.fft(green_complex, axis=1)
    result = 1j * jnp.fft.ifft(times * screen_complex, axis=1)
    return jnp.stack([jnp.real(result), jnp.imag(result)], axis=1).astype(jnp.bfloat16)


def reference(green_window, screened, retarded, energy_order, window_start):
    inverse = jnp.argsort(energy_order).astype(jnp.int32)
    order = energy_order.astype(jnp.int32)
    block_count = green_window.shape[3]

    def one_row(row):
        green_row = lax.dynamic_index_in_dim(green_window, row, 3, keepdims=False)
        green_row = jnp.take(green_row, inverse, axis=2).astype(jnp.float32)
        screen_row = lax.dynamic_index_in_dim(screened, row, 3, keepdims=False).astype(jnp.float32)
        sigma_true = convolve_row(green_row, screen_row)
        return jnp.take(sigma_true, order, axis=2)

    sigma_rows = lax.map(one_row, jnp.arange(block_count, dtype=jnp.int32))
    zero_row = jnp.zeros_like(sigma_rows[:1])
    padded = jnp.concatenate([zero_row, sigma_rows, zero_row], axis=0)

    def density_row(row):
        nearby = lax.dynamic_slice_in_dim(padded, row, 3, 0).astype(jnp.float32)
        nearby = nearby.reshape(3, 2, 2, NE, SLAB, SLAB)
        coupling = lax.dynamic_index_in_dim(retarded, row, 2, keepdims=False).astype(jnp.float32)
        dens_re = jnp.zeros((2, NE, B), jnp.float32)
        dens_im = jnp.zeros((2, NE, B), jnp.float32)
        for neighbour in range(3):
            part_re = nearby[neighbour, :, 0]
            part_im = nearby[neighbour, :, 1]
            right_re = coupling[0, :, neighbour]
            right_im = coupling[1, :, neighbour]
            inner_re = jnp.einsum("gepq,epa->geqa", part_re, right_re) - jnp.einsum("gepq,epa->geqa", part_im, right_im)
            inner_im = jnp.einsum("gepq,epa->geqa", part_re, right_im) + jnp.einsum("gepq,epa->geqa", part_im, right_re)
            dens_re = dens_re + jnp.sum(inner_re * right_re[None] + inner_im * right_im[None], axis=2)
            dens_im = dens_im + jnp.sum(inner_im * right_re[None] - inner_re * right_im[None], axis=2)
        own = nearby[1]
        diagonal_part = jnp.diagonal(own, axis1=3, axis2=4)
        start = window_start[row]
        column_ids = lax.broadcasted_iota(jnp.int32, (SLAB, B), 1)
        window_ids = lax.broadcasted_iota(jnp.int32, (SLAB, B), 0)
        place = (column_ids == window_ids + start).astype(jnp.float32)
        direct = jnp.einsum("gcep,pa->gcea", diagonal_part, place, precision=lax.Precision.HIGHEST)
        return jnp.stack([dens_re, dens_im], axis=1) + direct

    result = lax.map(density_row, jnp.arange(block_count, dtype=jnp.int32))
    return jnp.transpose(result, (1, 2, 3, 0, 4))
```

```python
import functools
import math

import jax
import jax.numpy as jnp
from jax import lax
from jax.experimental import pallas as pl
from jax.experimental.pallas import tpu as pltpu
from jax.sharding import PartitionSpec as P

F32 = jnp.float32
BF16 = jnp.bfloat16
VMEM = pl.BlockSpec(memory_space=pltpu.VMEM)
SMEM = pl.BlockSpec(memory_space=pltpu.SMEM)


def call(kernel, out_shape, in_specs, flops, scratch=()):
    return pl.pallas_call(
        kernel,
        out_shape=out_shape,
        in_specs=in_specs,
        out_specs=VMEM,
        scratch_shapes=list(scratch),
        compiler_params=pltpu.CompilerParams(vmem_limit_bytes=16 * 2**20),
        cost_estimate=pl.CostEstimate(flops=flops, bytes_accessed=2**20, transcendentals=0),
    )


def pack_kernel(devices, green_ref, out_ref):
    pairs, slots, entries = green_ref.shape
    columns = entries // devices
    rows = pairs * slots
    whole = jnp.concatenate([green_ref[at].astype(F32) for at in range(pairs)], axis=0)
    for at in range(devices):
        out_ref[at * rows : (at + 1) * rows, :] = whole[:, at * columns : (at + 1) * columns].astype(BF16)


def split_high_low(values):
    high = values.astype(BF16)
    return high, (values - high.astype(F32)).astype(BF16)


def convolve_kernel(first_ref, second_ref, spread_ref, screen_ref, out_ref):
    total = screen_ref.shape[0] // 4
    first_high, first_low = split_high_low(first_ref[...])
    spread = spread_ref[...]
    times = jnp.dot(
        jnp.concatenate([first_high, first_low], axis=1),
        jnp.concatenate([spread, spread], axis=0),
        preferred_element_type=F32,
    )
    screen = screen_ref[...].astype(F32)
    mixed = []
    for kind in range(2):
        base = kind * 2 * total
        times_re, times_im = times[base : base + total], times[base + total : base + 2 * total]
        screen_re, screen_im = screen[base : base + total], screen[base + total : base + 2 * total]
        mixed.append(times_re * screen_re - times_im * screen_im)
        mixed.append(times_re * screen_im + times_im * screen_re)
    mixed_high, mixed_low = split_high_low(jnp.concatenate(mixed, axis=0))
    second_high, second_low = split_high_low(second_ref[...])
    sigma = jnp.dot(
        jnp.concatenate([second_high, second_low, second_high], axis=1),
        jnp.concatenate([mixed_high, mixed_high, mixed_low], axis=0),
        preferred_element_type=F32,
    )
    out_ref[...] = sigma.astype(BF16)


def row_positions(slab, devices, shape):
    at = lax.broadcasted_iota(jnp.int32, shape, 0)
    return at % devices * (slab // devices) + at // devices


def to_tiles(tiles_ref, values):
    lanes = values.shape[1]
    for tile in range(tiles_ref.shape[0]):
        last = min(lanes, 128 * (tile + 1))
        tiles_ref[tile, :, : last - 128 * tile] = values[:, 128 * tile : last]


def strided_rows(tiles_ref, start, count, stride, lanes):
    found = [tiles_ref[tile, pl.ds(start, count, stride=stride), :] for tile in range(tiles_ref.shape[0])]
    return jnp.concatenate(found, axis=1)[:, :lanes]


def spread_rows(sigma_ref, wide_ref, slab, devices):
    to_tiles(wide_ref, sigma_ref[...].astype(F32))
    each = sigma_ref.shape[0] // devices
    depth = slab // devices
    matrices = []
    for at in range(each):
        flat = strided_rows(wide_ref, at, devices, each, slab * depth)
        matrices.append(
            jnp.concatenate([flat[:, slab * i : slab * (i + 1)] for i in range(depth)], axis=0)
        )
    return matrices


def neighbour_density(matrices, right_re, right_im, slot, slab, devices, scratch_ref):
    depth = slab // devices
    width = right_re.shape[1]
    shuffled = []
    for right in (right_re, right_im):
        to_tiles(scratch_ref, right.astype(F32))
        chunks = [strided_rows(scratch_ref, i, devices, depth, width) for i in range(depth)]
        shuffled.append(jnp.concatenate(chunks, axis=0))
    left = jnp.concatenate(
        [
            jnp.concatenate([matrices[slot * 4 + kind * 2], matrices[slot * 4 + kind * 2 + 1]], axis=1)
            for kind in range(2)
        ],
        axis=0,
    ).astype(BF16)
    inner_re = jnp.dot(left, jnp.concatenate([right_re, right_im], axis=0), preferred_element_type=F32)
    inner_im = jnp.dot(left, jnp.concatenate([-right_im, right_re], axis=0), preferred_element_type=F32)
    result = []
    for kind in range(2):
        z_re = inner_re[kind * slab : (kind + 1) * slab]
        z_im = inner_im[kind * slab : (kind + 1) * slab]
        result.append(
            (
                jnp.sum(z_re * shuffled[0] - z_im * shuffled[1], axis=0, keepdims=True),
                jnp.sum(z_re * shuffled[1] + z_im * shuffled[0], axis=0, keepdims=True),
            )
        )
    return result


def density_own_kernel(devices, start_ref, which_ref, sigma_ref, side_ref, retarded_ref, out_ref, wide_ref, scratch_ref):
    slots, slab, width = retarded_ref.shape[1], retarded_ref.shape[3], retarded_ref.shape[4]
    own = spread_rows(sigma_ref, wide_ref, slab, devices)
    side = spread_rows(side_ref, wide_ref, slab, devices)
    on_diagonal = row_positions(slab, devices, (slab, slab)) == lax.broadcasted_iota(jnp.int32, (slab, slab), 1)
    place = row_positions(slab, devices, (slab, width)) + start_ref[0] == lax.broadcasted_iota(
        jnp.int32, (slab, width), 1
    )
    which = which_ref[0]
    for slot in range(slots):
        first = neighbour_density(own, retarded_ref[0, slot, 1], retarded_ref[1, slot, 1], slot, slab, devices, scratch_ref)
        second = neighbour_density(side, retarded_ref[0, slot, which], retarded_ref[1, slot, which], slot, slab, devices, scratch_ref)
        for kind in range(2):
            for part in range(2):
                matrix = own[slot * 4 + kind * 2 + part]
                column = jnp.sum(jnp.where(on_diagonal, matrix, 0.0), axis=1, keepdims=True)
                direct = jnp.sum(jnp.where(place, column, 0.0), axis=0, keepdims=True)
                out_ref[kind * 2 + part, slot : slot + 1, :] = first[kind][part] + second[kind][part] + direct


def density_far_kernel(devices, which_ref, sigma_ref, retarded_ref, before_ref, out_ref, wide_ref, scratch_ref):
    slots, slab = retarded_ref.shape[1], retarded_ref.shape[3]
    far = spread_rows(sigma_ref, wide_ref, slab, devices)
    which = which_ref[0]
    for slot in range(slots):
        found = neighbour_density(far, retarded_ref[0, slot, which], retarded_ref[1, slot, which], slot, slab, devices, scratch_ref)
        for kind in range(2):
            for part in range(2):
                row = kind * 2 + part
                out_ref[row, slot : slot + 1, :] = before_ref[row, slot : slot + 1, :] + found[kind][part]


def phases(energy, time, quarter, count):
    turns = (4 * energy * time + count * quarter) % (4 * count)
    return jnp.cos(turns.astype(F32) * (2.0 * math.pi / (4 * count)))


def tables(energy_order, devices, slots):
    total = devices * slots
    size = 4 * total
    row = lax.broadcasted_iota(jnp.int32, (size, size), 0)
    col = lax.broadcasted_iota(jnp.int32, (size, size), 1)
    order = energy_order.reshape(devices, 1, 1, slots)
    energy = jnp.broadcast_to(order, (devices, 2, 2, slots)).reshape(1, size)
    same = row // (2 * total) == col // (2 * slots) % 2
    quarter = row // total % 2 - col // slots % 2
    first = jnp.where(same, phases(energy, row % total, quarter, total), 0.0)
    energy = jnp.broadcast_to(energy_order.reshape(total, 1), (total, 4)).reshape(size, 1)
    same = row // 2 % 2 == col // (2 * total)
    quarter = 1 - row % 2 + col // total % 2
    second = jnp.where(same, phases(energy, col % total, quarter, total), 0.0) * (1.0 / total)
    return first, second


def shards(green_window, screened, retarded, energy_order, window_start):
    devices = lax.axis_size("energy")
    rows = lax.axis_size("rows")
    slots, entries = green_window.shape[2], green_window.shape[4]
    slab, width = retarded.shape[4], retarded.shape[5]
    total = devices * slots
    columns = entries // devices
    flat = jax.ShapeDtypeStruct((4 * total, columns), BF16)

    packed = call(functools.partial(pack_kernel, devices), flat, [VMEM], 1000)(
        green_window.reshape(4, slots, entries)
    )
    spread = lax.all_to_all(packed, "energy", split_axis=0, concat_axis=0, tiled=True)
    first, second = tables(energy_order, devices, slots)
    sigma = call(convolve_kernel, flat, [VMEM] * 4, 2 * 5 * 16 * total * total * columns)(
        first, second, spread, screened.reshape(4 * total, columns)
    )
    returned = lax.all_to_all(sigma, "energy", split_axis=0, concat_axis=0, tiled=True)

    def trade(first_row):
        pairs = []
        for low in range(first_row, rows - 1, 2):
            pairs += [(low, low + 1), (low + 1, low)]
        return lax.ppermute(returned, "rows", pairs)

    far = trade(1)
    near = trade(0)
    odd = lax.axis_index("rows") % 2
    near_block = (2 - 2 * odd).astype(jnp.int32).reshape(1)
    far_block = (2 * odd).astype(jnp.int32).reshape(1)
    blocks = retarded.reshape(2, slots, 3, slab, width)
    scratch = [pltpu.VMEM((pl.cdiv(columns, 128), 4 * total, 128), F32), pltpu.VMEM((pl.cdiv(width, 128), slab, 128), F32)]
    out = jax.ShapeDtypeStruct((4, slots, width), F32)
    work = 2 * 8 * slots * 2 * slab * slab * width
    density = call(functools.partial(density_own_kernel, devices), out, [SMEM, SMEM] + [VMEM] * 3, 2 * work, scratch)(
        window_start, near_block, returned, near, blocks
    )
    density = call(functools.partial(density_far_kernel, devices), out, [SMEM] + [VMEM] * 3, work, scratch)(
        far_block, far, blocks, density
    )
    return density.reshape(2, 2, slots, 1, width)


def solution(mesh):
    in_specs = (
        P(None, None, "energy", "rows", None),
        P(None, None, None, "rows", "energy"),
        P(None, "energy", "rows", None, None, None),
        P(),
        P("rows"),
    )
    out_specs = P(None, None, "energy", "rows", None)
    return jax.shard_map(shards, mesh=mesh, in_specs=in_specs, out_specs=out_specs, check_vma=False)
```

```python
import functools
import math

import jax
import jax.numpy as jnp
from jax import lax
from jax.experimental import pallas as pl
from jax.experimental.pallas import tpu as pltpu
from jax.sharding import PartitionSpec as P

F32 = jnp.float32
BF16 = jnp.bfloat16
VMEM = pl.BlockSpec(memory_space=pltpu.VMEM)
SMEM = pl.BlockSpec(memory_space=pltpu.SMEM)


def call(kernel, out_shape, in_specs, flops, scratch=()):
    return pl.pallas_call(
        kernel,
        out_shape=out_shape,
        in_specs=in_specs,
        out_specs=jax.tree.map(lambda _: VMEM, out_shape),
        scratch_shapes=list(scratch),
        compiler_params=pltpu.CompilerParams(vmem_limit_bytes=16 * 2**20),
        cost_estimate=pl.CostEstimate(flops=flops, bytes_accessed=2**20, transcendentals=0),
    )


def pack_kernel(devices, green_ref, out_ref):
    pairs, slots, entries = green_ref.shape
    columns = entries // devices
    rows = pairs * slots
    whole = jnp.concatenate([green_ref[at].astype(F32) for at in range(pairs)], axis=0)
    for at in range(devices):
        out_ref[at * rows : (at + 1) * rows, :] = whole[:, at * columns : (at + 1) * columns].astype(BF16)


def split_high_low(values):
    high = values.astype(BF16)
    return high, (values - high.astype(F32)).astype(BF16)


def convolve_kernel(first_ref, second_ref, spread_ref, screen_ref, out_ref):
    total = screen_ref.shape[0] // 4
    first_high, first_low = split_high_low(first_ref[...])
    spread = spread_ref[...]
    times = jnp.dot(
        jnp.concatenate([first_high, first_low], axis=1),
        jnp.concatenate([spread, spread], axis=0),
        preferred_element_type=F32,
    )
    screen = screen_ref[...].astype(F32)
    mixed = []
    for kind in range(2):
        base = kind * 2 * total
        times_re, times_im = times[base : base + total], times[base + total : base + 2 * total]
        screen_re, screen_im = screen[base : base + total], screen[base + total : base + 2 * total]
        mixed.append(times_re * screen_re - times_im * screen_im)
        mixed.append(times_re * screen_im + times_im * screen_re)
    mixed_high, mixed_low = split_high_low(jnp.concatenate(mixed, axis=0))
    second_high, second_low = split_high_low(second_ref[...])
    sigma = jnp.dot(
        jnp.concatenate([second_high, second_low, second_high], axis=1),
        jnp.concatenate([mixed_high, mixed_high, mixed_low], axis=0),
        preferred_element_type=F32,
    )
    out_ref[0] = sigma.astype(BF16)
    out_ref[1] = sigma.astype(BF16)


def row_positions(slab, devices, shape):
    at = lax.broadcasted_iota(jnp.int32, shape, 0)
    return at % devices * (slab // devices) + at // devices


def to_tiles(tiles_ref, values):
    lanes = values.shape[1]
    for tile in range(tiles_ref.shape[0]):
        last = min(lanes, 128 * (tile + 1))
        tiles_ref[tile, :, : last - 128 * tile] = values[:, 128 * tile : last]


def strided_rows(tiles_ref, start, count, stride, lanes):
    found = [tiles_ref[tile, pl.ds(start, count, stride=stride), :] for tile in range(tiles_ref.shape[0])]
    return jnp.concatenate(found, axis=1)[:, :lanes]


def spread_rows(sigma_ref, wide_ref, slab, devices):
    to_tiles(wide_ref, sigma_ref[...].astype(F32))
    each = sigma_ref.shape[0] // devices
    depth = slab // devices
    matrices = []
    for at in range(each):
        flat = strided_rows(wide_ref, at, devices, each, slab * depth)
        matrices.append(
            jnp.concatenate([flat[:, slab * i : slab * (i + 1)] for i in range(depth)], axis=0)
        )
    return matrices


def prepare_kernel(devices, start_ref, blocks_ref, right_ref, shuffled_ref, place_ref, scratch_ref):
    slots, count, slab, width = blocks_ref.shape[1:]
    depth = slab // devices
    place_ref[...] = jnp.where(
        row_positions(slab, devices, (slab, width)) + start_ref[0]
        == lax.broadcasted_iota(jnp.int32, (slab, width), 1),
        1.0,
        0.0,
    )
    for slot in range(slots):
        for block in range(count):
            real, imag = blocks_ref[0, slot, block], blocks_ref[1, slot, block]
            right_ref[slot, block, 0, :slab, :] = real
            right_ref[slot, block, 0, slab:, :] = imag
            right_ref[slot, block, 1, :slab, :] = -imag
            right_ref[slot, block, 1, slab:, :] = real
            for part, values in enumerate((real, imag)):
                to_tiles(scratch_ref, values.astype(F32))
                for i in range(depth):
                    shuffled_ref[slot, block, part, i * devices : (i + 1) * devices, :] = strided_rows(
                        scratch_ref, i, devices, depth, width
                    )


def neighbour_density(matrices, right_ref, shuffled_ref, slot, block, slab):
    left = jnp.concatenate(
        [
            jnp.concatenate([matrices[slot * 4 + kind * 2], matrices[slot * 4 + kind * 2 + 1]], axis=1)
            for kind in range(2)
        ],
        axis=0,
    ).astype(BF16)
    inner_re = jnp.dot(left, right_ref[slot, block, 0], preferred_element_type=F32)
    inner_im = jnp.dot(left, right_ref[slot, block, 1], preferred_element_type=F32)
    wide_re, wide_im = shuffled_ref[slot, block, 0], shuffled_ref[slot, block, 1]
    result = []
    for kind in range(2):
        z_re = inner_re[kind * slab : (kind + 1) * slab]
        z_im = inner_im[kind * slab : (kind + 1) * slab]
        result.append(
            (
                jnp.sum(z_re * wide_re - z_im * wide_im, axis=0, keepdims=True),
                jnp.sum(z_re * wide_im + z_im * wide_re, axis=0, keepdims=True),
            )
        )
    return result


def density_kernel(devices, rows, sigma_ref, right_ref, shuffled_ref, place_ref, out_ref, wide_ref):
    slots, slab = shuffled_ref.shape[0], shuffled_ref.shape[3]
    row = lax.axis_index("rows")
    even = 1 - lax.rem(row, 2)
    has_far = jnp.where(jnp.logical_and(row > 0, row < rows - 1), 1.0, 0.0)
    own = spread_rows(sigma_ref.at[even], wide_ref, slab, devices)
    far = spread_rows(sigma_ref.at[1 - even], wide_ref, slab, devices)
    on_diagonal = row_positions(slab, devices, (slab, slab)) == lax.broadcasted_iota(jnp.int32, (slab, slab), 1)
    place = place_ref[...]
    for slot in range(slots):
        here = neighbour_density(own, right_ref, shuffled_ref, slot, 1, slab)
        there = neighbour_density(far, right_ref, shuffled_ref, slot, 2 - 2 * even, slab)
        for kind in range(2):
            for part in range(2):
                matrix = own[slot * 4 + kind * 2 + part]
                column = jnp.sum(jnp.where(on_diagonal, matrix, 0.0), axis=1, keepdims=True)
                direct = jnp.sum(place * column, axis=0, keepdims=True)
                out_ref[(kind * 2 + part) * slots + slot] = here[kind][part] + there[kind][part] * has_far + direct


def density_near_kernel(devices, sigma_ref, right_ref, shuffled_ref, before_ref, out_ref, wide_ref):
    slots, slab = shuffled_ref.shape[0], shuffled_ref.shape[3]
    near = spread_rows(sigma_ref, wide_ref, slab, devices)
    block = 2 - 2 * lax.rem(lax.axis_index("rows"), 2)
    for slot in range(slots):
        found = neighbour_density(near, right_ref, shuffled_ref, slot, block, slab)
        for kind in range(2):
            for part in range(2):
                at = (kind * 2 + part) * slots + slot
                out_ref[at] = before_ref[at] + found[kind][part]


def phases(energy, time, quarter, count):
    turns = (4 * energy * time + count * quarter) % (4 * count)
    return jnp.cos(turns.astype(F32) * (2.0 * math.pi / (4 * count)))


def tables(energy_order, devices, slots):
    total = devices * slots
    size = 4 * total
    row = lax.broadcasted_iota(jnp.int32, (size, size), 0)
    col = lax.broadcasted_iota(jnp.int32, (size, size), 1)
    order = energy_order.reshape(devices, 1, 1, slots)
    energy = jnp.broadcast_to(order, (devices, 2, 2, slots)).reshape(1, size)
    same = row // (2 * total) == col // (2 * slots) % 2
    quarter = row // total % 2 - col // slots % 2
    first = jnp.where(same, phases(energy, row % total, quarter, total), 0.0)
    energy = jnp.broadcast_to(energy_order.reshape(total, 1), (total, 4)).reshape(size, 1)
    same = row // 2 % 2 == col // (2 * total)
    quarter = 1 - row % 2 + col // total % 2
    second = jnp.where(same, phases(energy, col % total, quarter, total), 0.0) * (1.0 / total)
    return first, second


def shards(green_window, screened, retarded, energy_order, window_start):
    devices = lax.axis_size("energy")
    rows = lax.axis_size("rows")
    slots, entries = green_window.shape[2], green_window.shape[4]
    slab, width = retarded.shape[4], retarded.shape[5]
    total = devices * slots
    columns = entries // devices
    flat = jax.ShapeDtypeStruct((4 * total, columns), BF16)

    packed = call(functools.partial(pack_kernel, devices), flat, [VMEM], 1000)(
        green_window.reshape(4, slots, entries)
    )
    spread = lax.all_to_all(packed, "energy", split_axis=0, concat_axis=0, tiled=True)
    first, second = tables(energy_order, devices, slots)
    right, shuffled, place = call(
        functools.partial(prepare_kernel, devices),
        (
            jax.ShapeDtypeStruct((slots, 3, 2, 2 * slab, width), BF16),
            jax.ShapeDtypeStruct((slots, 3, 2, slab, width), F32),
            jax.ShapeDtypeStruct((slab, width), F32),
        ),
        [SMEM, VMEM],
        10**6,
        [pltpu.VMEM((pl.cdiv(width, 128), slab, 128), F32)],
    )(window_start, retarded.reshape(2, slots, 3, slab, width))
    spread, right, shuffled, place = lax.optimization_barrier((spread, right, shuffled, place))
    sigma = call(
        convolve_kernel,
        jax.ShapeDtypeStruct((2, 4 * total, columns), BF16),
        [VMEM] * 4,
        2 * 5 * 16 * total * total * columns,
    )(first, second, spread, screened.reshape(4 * total, columns))

    odd = lax.axis_index("rows") % 2 == 1
    sigma, odd = lax.optimization_barrier((sigma, odd))

    groups = [
        [energy * rows + row % rows for row in (low, low + 1) for energy in range(devices)]
        for low in range(1, rows, 2)
    ]
    both = lax.all_to_all(
        sigma.reshape(2 * devices, 4 * slots, columns),
        ("energy", "rows"),
        split_axis=0,
        concat_axis=0,
        tiled=True,
        axis_index_groups=groups,
    ).reshape(2, 4 * total, columns)
    own = jnp.where(odd, both[0], both[1])
    pairs = [(row, row ^ 1) for row in range(rows)]
    near = lax.ppermute(own, "rows", pairs)

    scratch = [pltpu.VMEM((pl.cdiv(columns, 128), 4 * total, 128), F32)]
    out = jax.ShapeDtypeStruct((4 * slots, 1, width), F32)
    work = 2 * 8 * slots * 2 * slab * slab * width
    density = call(functools.partial(density_kernel, devices, rows), out, [VMEM] * 4, 2 * work, scratch)(
        both, right, shuffled, place
    )
    density = call(functools.partial(density_near_kernel, devices), out, [VMEM] * 4, work, scratch)(
        near, right, shuffled, density
    )
    return density.reshape(2, 2, slots, 1, width)


def solution(mesh):
    in_specs = (
        P(None, None, "energy", "rows", None),
        P(None, None, None, "rows", "energy"),
        P(None, "energy", "rows", None, None, None),
        P(),
        P("rows"),
    )
    out_specs = P(None, None, "energy", "rows", None)
    return jax.shard_map(shards, mesh=mesh, in_specs=in_specs, out_specs=out_specs, check_vma=False)
```

```python
import functools
import math

import jax
import jax.numpy as jnp
import numpy as np
from jax import lax
from jax.experimental import pallas as pl
from jax.experimental.pallas import tpu as pltpu
from jax.sharding import PartitionSpec as P

F32 = jnp.float32
BF16 = jnp.bfloat16
VMEM = pl.BlockSpec(memory_space=pltpu.VMEM)
SMEM = pl.BlockSpec(memory_space=pltpu.SMEM)
HBM = pl.BlockSpec(memory_space=pltpu.HBM)


def call(kernel, out_shape, in_specs, flops, scratch=(), moved=2**20):
    return pl.pallas_call(
        kernel,
        out_shape=out_shape,
        in_specs=in_specs,
        out_specs=jax.tree.map(lambda _: VMEM, out_shape),
        scratch_shapes=list(scratch),
        compiler_params=pltpu.CompilerParams(vmem_limit_bytes=16 * 2**20),
        cost_estimate=pl.CostEstimate(flops=flops, bytes_accessed=moved, transcendentals=0),
    )


def middle_of(count):
    return (count // 2 + 1) % count


def exchange_order(count):
    return [(middle_of(count) - at) % count for at in range(count)]


def shuffled_orders(count):
    draws = np.random.RandomState(20)
    first, second = ([int(at) for at in draws.permutation(count)] for _ in range(2))
    middle = middle_of(count)
    return [[middle] + [at for at in first if at != middle], second]


def split_high_low(values):
    high = values.astype(BF16)
    return high, (values - high.astype(F32)).astype(BF16)


def wrap(values, count):
    return values & (count - 1) if count & (count - 1) == 0 else values % count


def parts_of(values, count):
    return values >> (count.bit_length() - 1) if count & (count - 1) == 0 else values // count


def phases(energy, time, quarter, count):
    turns = wrap(4 * energy * time + count * quarter, 4 * count)
    half = jnp.where(turns >= 2 * count, turns - 2 * count, turns)
    odd = half >= count
    angle = jnp.where(odd, half - count, half).astype(F32) * (0.5 * math.pi / count)
    square = angle * angle
    cosine, sine = 0.0, 0.0
    for power in range(7, -1, -1):
        cosine = cosine * square + (-1) ** power / math.factorial(2 * power)
        sine = sine * square + (-1) ** power / math.factorial(2 * power + 1)
    value = jnp.where(odd, -sine * angle, cosine)
    return jnp.where(turns >= 2 * count, -value, value)


def tables(energy_order, order, back_order):
    total = energy_order.shape[1]
    slots = total // len(order)
    size = 4 * total
    row = lax.broadcasted_iota(jnp.int32, (size, 1), 0)
    col = lax.broadcasted_iota(jnp.int32, (1, size), 1)

    def device_at(place, places):
        found = jnp.zeros_like(place)
        for at, device in enumerate(places):
            found = jnp.where(place == at, device, found)
        return found

    across = lax.broadcasted_iota(jnp.int32, (total, total), 1)
    down = lax.broadcasted_iota(jnp.int32, (total, total), 0)
    energy_down = jnp.sum(jnp.where(across == down, energy_order, 0), axis=1, keepdims=True)

    source = device_at(parts_of(col, 4 * slots), order) * slots + wrap(col, slots)
    energy = jnp.sum(
        jnp.where(lax.broadcasted_iota(jnp.int32, (total, size), 0) == source, energy_down, 0), axis=0, keepdims=True
    )
    same = parts_of(row, 2 * total) == wrap(parts_of(col, 2 * slots), 2)
    quarter = wrap(parts_of(row, total), 2) - wrap(parts_of(col, slots), 2)
    first = jnp.where(same, phases(energy, wrap(row, total), quarter, total), 0.0)
    source = device_at(parts_of(row, 4 * slots), back_order) * slots + wrap(parts_of(row, 4), slots)
    energy = jnp.sum(
        jnp.where(lax.broadcasted_iota(jnp.int32, (size, total), 1) == source, energy_order, 0), axis=1, keepdims=True
    )
    same = wrap(parts_of(row, 2), 2) == parts_of(col, 2 * total)
    quarter = 1 - wrap(row, 2) + wrap(parts_of(col, total), 2)
    second = jnp.where(same, phases(energy, wrap(col, total), quarter, total), 0.0) * (1.0 / total)
    return first, second


def row_positions(slab, devices, shape):
    at = lax.broadcasted_iota(jnp.int32, shape, 0)
    return wrap(at, devices) * (slab // devices) + parts_of(at, devices)


def to_tiles(tiles_ref, values, start=0):
    rows, lanes = values.shape
    for tile in range(tiles_ref.shape[0]):
        last = min(lanes, 128 * (tile + 1))
        tiles_ref[tile, pl.ds(start, rows), : last - 128 * tile] = values[:, 128 * tile : last]


def strided_rows(tiles_ref, start, count, stride, lanes):
    found = [tiles_ref[tile, pl.ds(start, count, stride=stride), :] for tile in range(tiles_ref.shape[0])]
    return jnp.concatenate(found, axis=1)[:, :lanes]


def front_kernel(
    order,
    back_order,
    energy_hbm,
    green_hbm,
    out_ref,
    first_ref,
    second_ref,
    energy_ref,
    green_ref,
    sems,
):
    pairs = ((energy_hbm, energy_ref), (green_hbm, green_ref))
    copies = [pltpu.make_async_copy(source, target, sems.at[at]) for at, (source, target) in enumerate(pairs)]
    for copy in copies:
        copy.start()
    copies[0].wait()
    first, second = tables(energy_ref[...], order, back_order)
    first_high, first_low = split_high_low(first)
    second_high, second_low = split_high_low(second)
    first_ref[...] = jnp.concatenate([first_high, first_low], axis=1)
    second_ref[...] = jnp.concatenate([second_high, second_low, second_high], axis=1)
    copies[1].wait()
    pairs, slots, entries = green_ref.shape
    columns = entries // len(order)
    rows = pairs * slots
    whole = jnp.concatenate([green_ref[at].astype(F32) for at in range(pairs)], axis=0)
    for at, device in enumerate(order):
        out_ref[at * rows : (at + 1) * rows, :] = whole[:, device * columns : (device + 1) * columns].astype(BF16)


def prepare_block(real, imag, right_ref, shuffled_ref, scratch_ref, devices):
    slab, width = real.shape
    padded = right_ref.shape[1] // 2
    depth = slab // devices
    gap = jnp.zeros((padded - slab, width), BF16)
    for half, (upper, lower) in enumerate(((real, imag), (-imag, real))):
        right_ref[half, :slab, :] = upper
        right_ref[half, slab:padded, :] = gap
        right_ref[half, padded : padded + slab, :] = lower
        right_ref[half, padded + slab :, :] = gap
    for part, values in enumerate((real, imag)):
        to_tiles(scratch_ref, values.astype(F32))
        for i in range(depth):
            shuffled_ref[part, i * devices : (i + 1) * devices, :] = strided_rows(
                scratch_ref, i, devices, depth, width
            )


def convolve_kernel(orders, first_ref, second_ref, spread_ref, screen_ref, out_ref):
    total = screen_ref.shape[0] // 4
    spread = spread_ref[...]
    times = jnp.dot(first_ref[...], jnp.concatenate([spread, spread], axis=0), preferred_element_type=F32)
    screen = screen_ref[...].astype(F32)
    mixed = []
    for kind in range(2):
        base = kind * 2 * total
        times_re, times_im = times[base : base + total], times[base + total : base + 2 * total]
        screen_re, screen_im = screen[base : base + total], screen[base + total : base + 2 * total]
        mixed.append(times_re * screen_re - times_im * screen_im)
        mixed.append(times_re * screen_im + times_im * screen_re)
    mixed_high, mixed_low = split_high_low(jnp.concatenate(mixed, axis=0))
    sigma = jnp.dot(
        second_ref[...],
        jnp.concatenate([mixed_high, mixed_high, mixed_low], axis=0),
        preferred_element_type=F32,
    )
    each = sigma.shape[0] // len(orders[0])
    chunks = {device: sigma[at * each : (at + 1) * each] for at, device in enumerate(orders[0])}
    for side, order in enumerate(orders):
        out_ref[side] = jnp.concatenate([chunks[device] for device in order], axis=0).astype(BF16)


def spread_rows(sigma_ref, wide_ref, slab, padded, places):
    devices = len(places)
    each = sigma_ref.shape[0] // devices
    depth = slab // devices
    wide = sigma_ref[...].astype(F32)
    lanes = wide_ref.shape[0] * 128
    wide = jnp.concatenate([wide, jnp.zeros((wide.shape[0], lanes - wide.shape[1]), F32)], axis=1)
    for at, device in enumerate(places):
        to_tiles(wide_ref, wide[at * each : (at + 1) * each], device * each)
    matrices = []
    for at in range(each):
        flat = strided_rows(wide_ref, at, devices, each, lanes)
        matrices.append(
            jnp.concatenate([flat[:, slab * i : slab * i + padded] for i in range(depth)], axis=0)
        )
    return matrices


def neighbour_density(matrices, right_ref, shuffled_ref, slot):
    slab = shuffled_ref.shape[1]
    left = jnp.concatenate(
        [
            jnp.concatenate([matrices[slot * 4 + kind * 2], matrices[slot * 4 + kind * 2 + 1]], axis=1)
            for kind in range(2)
        ],
        axis=0,
    ).astype(BF16)
    inner_re = jnp.dot(left, right_ref[0], preferred_element_type=F32)
    inner_im = jnp.dot(left, right_ref[1], preferred_element_type=F32)
    wide_re, wide_im = shuffled_ref[0], shuffled_ref[1]
    result = []
    for kind in range(2):
        z_re = inner_re[kind * slab : (kind + 1) * slab]
        z_im = inner_im[kind * slab : (kind + 1) * slab]
        result.append((z_re * wide_re - z_im * wide_im, z_re * wide_im + z_im * wide_re))
    return result


def density_kernel(
    orders,
    rows,
    start_ref,
    sigma_ref,
    blocks_ref,
    out_ref,
    near_right_ref,
    near_shuffled_ref,
    wide_ref,
    scratch_ref,
    right_ref,
    shuffled_ref,
):
    slots, _, slab, width = blocks_ref.shape[1:]
    padded = right_ref.shape[3] // 2
    devices = len(orders[0])
    row = lax.axis_index("rows")
    odd = lax.rem(row, 2)
    keep = [jnp.where(row == 0, 0.0, 1.0), jnp.where(row == rows - 1, 0.0, 1.0)]
    sides = [spread_rows(sigma_ref.at[side], wide_ref, slab, padded, orders[side]) for side in range(2)]
    on_diagonal = row_positions(slab, devices, (slab, padded)) == lax.broadcasted_iota(jnp.int32, (slab, padded), 1)
    diagonal = jnp.concatenate(
        [
            jnp.sum(jnp.where(on_diagonal, jnp.where(odd == 1, upper, lower), 0.0), axis=0, keepdims=True)
            for upper, lower in zip(*sides)
        ],
        axis=0,
    )
    at_row = lax.broadcasted_iota(jnp.int32, (padded, width), 0)
    placed = at_row + start_ref[0] == lax.broadcasted_iota(jnp.int32, (padded, width), 1)
    place = jnp.where(jnp.logical_and(placed, at_row < slab), 1.0, 0.0).astype(BF16)
    direct = jnp.dot(diagonal.astype(BF16), place, preferred_element_type=F32)
    for slot in range(slots):
        found = []
        for side in range(2):
            block = side + odd
            mine = (right_ref.at[slot, side], shuffled_ref.at[slot, side])
            prepare_block(
                blocks_ref[0, slot, block], blocks_ref[1, slot, block], *mine, scratch_ref.at[slot, side], devices
            )
            found.append(neighbour_density(sides[side], *mine, slot))
        for kind in range(2):
            for part in range(2):
                at = slot * 4 + kind * 2 + part
                both = found[0][kind][part] * keep[0] + found[1][kind][part] * keep[1]
                out_ref[(kind * 2 + part) * slots + slot] = direct[at : at + 1] + jnp.sum(
                    both, axis=0, keepdims=True
                )
    for slot in range(slots):
        block = 2 - 2 * odd
        prepare_block(
            blocks_ref[0, slot, block],
            blocks_ref[1, slot, block],
            near_right_ref.at[slot],
            near_shuffled_ref.at[slot],
            scratch_ref.at[slot, 2],
            devices,
        )


def density_near_kernel(orders, sigma_ref, right_ref, shuffled_ref, before_ref, out_ref, wide_ref):
    slots, slab, padded = shuffled_ref.shape[0], shuffled_ref.shape[2], right_ref.shape[2] // 2
    odd = lax.rem(lax.axis_index("rows"), 2)
    places = [jnp.where(odd == 1, even_row, odd_row) for odd_row, even_row in zip(*orders)]
    near = spread_rows(sigma_ref, wide_ref, slab, padded, places)
    for slot in range(slots):
        found = neighbour_density(near, right_ref.at[slot], shuffled_ref.at[slot], slot)
        for kind in range(2):
            for part in range(2):
                at = (kind * 2 + part) * slots + slot
                out_ref[at] = before_ref[at] + jnp.sum(found[kind][part], axis=0, keepdims=True)


def shards(green_window, screened, retarded, energy_order, window_start):
    devices = lax.axis_size("energy")
    rows = lax.axis_size("rows")
    slots, entries = green_window.shape[2], green_window.shape[4]
    slab, width = retarded.shape[4], retarded.shape[5]
    total = devices * slots
    columns = entries // devices
    order = exchange_order(devices)
    orders = shuffled_orders(devices)
    padded = pl.cdiv(slab, 128) * 128

    def stay(values):
        return pltpu.with_memory_space_constraint(values, pltpu.HBM)

    packed, first, second = call(
        functools.partial(front_kernel, order, orders[0]),
        (
            jax.ShapeDtypeStruct((4 * total, columns), BF16),
            jax.ShapeDtypeStruct((4 * total, 2 * 4 * total), BF16),
            jax.ShapeDtypeStruct((4 * total, 3 * 4 * total), BF16),
        ),
        [HBM] * 2,
        1000,
        [
            pltpu.VMEM((1, total), jnp.int32),
            pltpu.VMEM((4, slots, entries), BF16),
            pltpu.SemaphoreType.DMA((2,)),
        ],
    )(stay(energy_order.reshape(1, total)), stay(green_window.reshape(4, slots, entries)))
    odd = lax.axis_index("rows") % 2 == 1
    packed, first, second, odd = lax.optimization_barrier((packed, first, second, odd))
    spread = lax.all_to_all(
        packed, "energy", split_axis=0, concat_axis=0, tiled=True, axis_index_groups=[order]
    )
    sigma = call(
        functools.partial(convolve_kernel, orders),
        jax.ShapeDtypeStruct((2, 4 * total, columns), BF16),
        [VMEM] * 4,
        2 * 5 * 16 * total * total * columns,
    )(first, second, spread, screened.reshape(4 * total, columns))

    groups = [
        [energy * rows + (low + side) % rows for side in range(2) for energy in orders[side]]
        for low in range(1, rows, 2)
    ]
    both = lax.all_to_all(
        sigma.reshape(2 * devices, 4 * slots, columns),
        ("energy", "rows"),
        split_axis=0,
        concat_axis=0,
        tiled=True,
        axis_index_groups=groups,
    ).reshape(2, 4 * total, columns)
    own = jnp.where(odd, both[0], both[1])
    pairs = [(row, row ^ 1) for row in range(rows)]
    near = lax.ppermute(own, "rows", pairs)

    spreading = pltpu.VMEM((pl.cdiv(columns + padded - slab, 128), 4 * total, 128), F32)
    out = jax.ShapeDtypeStruct((4 * slots, 1, width), F32)
    work = 2 * 8 * slots * 2 * slab * slab * width
    density, right, shuffled = call(
        functools.partial(density_kernel, orders, rows),
        (
            out,
            jax.ShapeDtypeStruct((slots, 2, 2 * padded, width), BF16),
            jax.ShapeDtypeStruct((slots, 2, slab, width), F32),
        ),
        [SMEM] + [VMEM] * 2,
        2 * work,
        [
            spreading,
            pltpu.VMEM((slots, 3, pl.cdiv(width, 128), slab, 128), F32),
            pltpu.VMEM((slots, 2, 2, 2 * padded, width), BF16),
            pltpu.VMEM((slots, 2, 2, slab, width), F32),
        ],
    )(window_start, both, retarded.reshape(2, slots, 3, slab, width))
    density = call(functools.partial(density_near_kernel, orders), out, [VMEM] * 4, work, [spreading])(
        near, right, shuffled, density
    )
    return density.reshape(2, 2, slots, 1, width)


def solution(mesh):
    in_specs = (
        P(None, None, "energy", "rows", None),
        P(None, None, None, "rows", "energy"),
        P(None, "energy", "rows", None, None, None),
        P(),
        P("rows"),
    )
    out_specs = P(None, None, "energy", "rows", None)
    return jax.shard_map(shards, mesh=mesh, in_specs=in_specs, out_specs=out_specs, check_vma=False)
```

```python
import functools
import math

import jax
import jax.numpy as jnp
from jax import lax
from jax.experimental import pallas as pl
from jax.experimental.pallas import tpu as pltpu
from jax.sharding import PartitionSpec as P

F32 = jnp.float32
BF16 = jnp.bfloat16
VMEM = pl.BlockSpec(memory_space=pltpu.VMEM)
SMEM = pl.BlockSpec(memory_space=pltpu.SMEM)
HBM = pl.BlockSpec(memory_space=pltpu.HBM)


def call(kernel, out_shape, in_specs, flops, scratch=(), moved=2**20):
    return pl.pallas_call(
        kernel,
        out_shape=out_shape,
        in_specs=in_specs,
        out_specs=jax.tree.map(lambda _: VMEM, out_shape),
        scratch_shapes=list(scratch),
        compiler_params=pltpu.CompilerParams(vmem_limit_bytes=16 * 2**20),
        cost_estimate=pl.CostEstimate(flops=flops, bytes_accessed=moved, transcendentals=0),
    )


def exchange_order(count):
    middle = count // 2 + 1
    return [(middle - at) % count for at in range(count)]


def split_high_low(values):
    high = values.astype(BF16)
    return high, (values - high.astype(F32)).astype(BF16)


def wrap(values, count):
    return values & (count - 1) if count & (count - 1) == 0 else values % count


def parts_of(values, count):
    return values >> (count.bit_length() - 1) if count & (count - 1) == 0 else values // count


def phases(energy, time, quarter, count):
    turns = wrap(4 * energy * time + count * quarter, 4 * count)
    half = jnp.where(turns >= 2 * count, turns - 2 * count, turns)
    odd = half >= count
    angle = jnp.where(odd, half - count, half).astype(F32) * (0.5 * math.pi / count)
    square = angle * angle
    cosine, sine = 0.0, 0.0
    for power in range(7, -1, -1):
        cosine = cosine * square + (-1) ** power / math.factorial(2 * power)
        sine = sine * square + (-1) ** power / math.factorial(2 * power + 1)
    value = jnp.where(odd, -sine * angle, cosine)
    return jnp.where(turns >= 2 * count, -value, value)


def tables(energy_order, order):
    total = energy_order.shape[1]
    slots = total // len(order)
    size = 4 * total
    row = lax.broadcasted_iota(jnp.int32, (size, 1), 0)
    col = lax.broadcasted_iota(jnp.int32, (1, size), 1)

    def device_at(place, places):
        found = jnp.zeros_like(place)
        for at, device in enumerate(places):
            found = jnp.where(place == at, device, found)
        return found

    across = lax.broadcasted_iota(jnp.int32, (total, total), 1)
    down = lax.broadcasted_iota(jnp.int32, (total, total), 0)
    energy_down = jnp.sum(jnp.where(across == down, energy_order, 0), axis=1, keepdims=True)

    source = device_at(parts_of(col, 4 * slots), order) * slots + wrap(col, slots)
    energy = jnp.sum(
        jnp.where(lax.broadcasted_iota(jnp.int32, (total, size), 0) == source, energy_down, 0), axis=0, keepdims=True
    )
    same = parts_of(row, 2 * total) == wrap(parts_of(col, 2 * slots), 2)
    quarter = wrap(parts_of(row, total), 2) - wrap(parts_of(col, slots), 2)
    first = jnp.where(same, phases(energy, wrap(row, total), quarter, total), 0.0)
    source = device_at(parts_of(row, 4 * slots), order) * slots + wrap(parts_of(row, 4), slots)
    energy = jnp.sum(
        jnp.where(lax.broadcasted_iota(jnp.int32, (size, total), 1) == source, energy_order, 0), axis=1, keepdims=True
    )
    same = wrap(parts_of(row, 2), 2) == parts_of(col, 2 * total)
    quarter = 1 - wrap(row, 2) + wrap(parts_of(col, total), 2)
    second = jnp.where(same, phases(energy, wrap(col, total), quarter, total), 0.0) * (1.0 / total)
    return first, second


def row_positions(slab, devices, shape):
    at = lax.broadcasted_iota(jnp.int32, shape, 0)
    return wrap(at, devices) * (slab // devices) + parts_of(at, devices)


def to_tiles(tiles_ref, values, start=0):
    rows, lanes = values.shape
    for tile in range(tiles_ref.shape[0]):
        last = min(lanes, 128 * (tile + 1))
        tiles_ref[tile, pl.ds(start, rows), : last - 128 * tile] = values[:, 128 * tile : last]


def strided_rows(tiles_ref, start, count, stride, lanes):
    found = [tiles_ref[tile, pl.ds(start, count, stride=stride), :] for tile in range(tiles_ref.shape[0])]
    return jnp.concatenate(found, axis=1)[:, :lanes]


def front_kernel(
    order,
    energy_hbm,
    green_hbm,
    out_ref,
    first_ref,
    second_ref,
    energy_ref,
    green_ref,
    sems,
):
    pairs = ((energy_hbm, energy_ref), (green_hbm, green_ref))
    copies = [pltpu.make_async_copy(source, target, sems.at[at]) for at, (source, target) in enumerate(pairs)]
    for copy in copies:
        copy.start()
    copies[0].wait()
    first, second = tables(energy_ref[...], order)
    first_high, first_low = split_high_low(first)
    second_high, second_low = split_high_low(second)
    first_ref[...] = jnp.concatenate([first_high, first_low], axis=1)
    second_ref[...] = jnp.concatenate([second_high, second_low, second_high], axis=1)
    copies[1].wait()
    pairs, slots, entries = green_ref.shape
    columns = entries // len(order)
    rows = pairs * slots
    whole = jnp.concatenate([green_ref[at].astype(F32) for at in range(pairs)], axis=0)
    for at, device in enumerate(order):
        out_ref[at * rows : (at + 1) * rows, :] = whole[:, device * columns : (device + 1) * columns].astype(BF16)


def convolve_kernel(first_ref, second_ref, spread_ref, screen_ref, out_ref):
    total = screen_ref.shape[0] // 4
    spread = spread_ref[...]
    times = jnp.dot(first_ref[...], jnp.concatenate([spread, spread], axis=0), preferred_element_type=F32)
    screen = screen_ref[...].astype(F32)
    mixed = []
    for kind in range(2):
        base = kind * 2 * total
        times_re, times_im = times[base : base + total], times[base + total : base + 2 * total]
        screen_re, screen_im = screen[base : base + total], screen[base + total : base + 2 * total]
        mixed.append(times_re * screen_re - times_im * screen_im)
        mixed.append(times_re * screen_im + times_im * screen_re)
    mixed_high, mixed_low = split_high_low(jnp.concatenate(mixed, axis=0))
    sigma = jnp.dot(
        second_ref[...],
        jnp.concatenate([mixed_high, mixed_high, mixed_low], axis=0),
        preferred_element_type=F32,
    ).astype(BF16)
    out_ref[0] = sigma
    out_ref[1] = sigma


def spread_rows(sigma_ref, wide_ref, slab, padded, places):
    devices = len(places)
    each = sigma_ref.shape[0] // devices
    depth = slab // devices
    wide = sigma_ref[...].astype(F32)
    lanes = wide_ref.shape[0] * 128
    wide = jnp.concatenate([wide, jnp.zeros((wide.shape[0], lanes - wide.shape[1]), F32)], axis=1)
    for at, device in enumerate(places):
        to_tiles(wide_ref, wide[at * each : (at + 1) * each], device * each)
    matrices = []
    for at in range(each):
        flat = strided_rows(wide_ref, at, devices, each, lanes)
        matrices.append(
            jnp.concatenate([flat[:, slab * i : slab * i + padded] for i in range(depth)], axis=0)
        )
    return matrices


def row_order(slab, devices):
    shape = (slab, slab)
    return jnp.where(
        row_positions(slab, devices, shape) == lax.broadcasted_iota(jnp.int32, shape, 1), 1.0, 0.0
    ).astype(BF16)


def neighbour_density(matrices, blocks_ref, slot, block, ordering):
    real, imag = blocks_ref[0, slot, block], blocks_ref[1, slot, block]
    slab, width = real.shape
    gap = jnp.zeros((matrices[0].shape[1] - slab, width), BF16)
    left = jnp.concatenate(
        [
            jnp.concatenate([matrices[slot * 4 + kind * 2], matrices[slot * 4 + kind * 2 + 1]], axis=1)
            for kind in range(2)
        ],
        axis=0,
    ).astype(BF16)
    inner_re = jnp.dot(left, jnp.concatenate([real, gap, imag, gap], axis=0), preferred_element_type=F32)
    inner_im = jnp.dot(left, jnp.concatenate([-imag, gap, real, gap], axis=0), preferred_element_type=F32)
    wide_re = jnp.dot(ordering, real, preferred_element_type=F32)
    wide_im = jnp.dot(ordering, imag, preferred_element_type=F32)
    result = []
    for kind in range(2):
        z_re = inner_re[kind * slab : (kind + 1) * slab]
        z_im = inner_im[kind * slab : (kind + 1) * slab]
        result.append((z_re * wide_re - z_im * wide_im, z_re * wide_im + z_im * wide_re))
    return result


def density_kernel(order, rows, padded, start_ref, sigma_ref, blocks_ref, out_ref, wide_ref):
    slots, _, slab, width = blocks_ref.shape[1:]
    devices = len(order)
    row = lax.axis_index("rows")
    odd = lax.rem(row, 2)
    has_far = jnp.where(jnp.logical_and(row > 0, row < rows - 1), 1.0, 0.0)
    own = spread_rows(sigma_ref.at[1 - odd], wide_ref.at[0], slab, padded, order)
    far = spread_rows(sigma_ref.at[odd], wide_ref.at[1], slab, padded, order)
    on_diagonal = row_positions(slab, devices, (slab, padded)) == lax.broadcasted_iota(jnp.int32, (slab, padded), 1)
    diagonal = jnp.concatenate(
        [jnp.sum(jnp.where(on_diagonal, matrix, 0.0), axis=0, keepdims=True) for matrix in own], axis=0
    )
    at_row = lax.broadcasted_iota(jnp.int32, (padded, width), 0)
    placed = at_row + start_ref[0] == lax.broadcasted_iota(jnp.int32, (padded, width), 1)
    place = jnp.where(jnp.logical_and(placed, at_row < slab), 1.0, 0.0).astype(BF16)
    direct = jnp.dot(diagonal.astype(BF16), place, preferred_element_type=F32)
    ordering = row_order(slab, devices)
    for slot in range(slots):
        here = neighbour_density(own, blocks_ref, slot, 1, ordering)
        there = neighbour_density(far, blocks_ref, slot, 2 * odd, ordering)
        for kind in range(2):
            for part in range(2):
                at = slot * 4 + kind * 2 + part
                out_ref[(kind * 2 + part) * slots + slot] = direct[at : at + 1] + jnp.sum(
                    here[kind][part] + there[kind][part] * has_far, axis=0, keepdims=True
                )


def density_near_kernel(order, padded, sigma_ref, blocks_ref, before_ref, out_ref, wide_ref):
    slots, _, slab, _ = blocks_ref.shape[1:]
    near = spread_rows(sigma_ref, wide_ref, slab, padded, order)
    ordering = row_order(slab, len(order))
    block = 2 - 2 * lax.rem(lax.axis_index("rows"), 2)
    for slot in range(slots):
        found = neighbour_density(near, blocks_ref, slot, block, ordering)
        for kind in range(2):
            for part in range(2):
                at = (kind * 2 + part) * slots + slot
                out_ref[at] = before_ref[at] + jnp.sum(found[kind][part], axis=0, keepdims=True)


def shards(green_window, screened, retarded, energy_order, window_start):
    devices = lax.axis_size("energy")
    rows = lax.axis_size("rows")
    slots, entries = green_window.shape[2], green_window.shape[4]
    slab, width = retarded.shape[4], retarded.shape[5]
    total = devices * slots
    columns = entries // devices
    order = exchange_order(devices)
    padded = pl.cdiv(slab, 128) * 128

    def stay(values):
        return pltpu.with_memory_space_constraint(values, pltpu.HBM)

    packed, first, second = call(
        functools.partial(front_kernel, order),
        (
            jax.ShapeDtypeStruct((4 * total, columns), BF16),
            jax.ShapeDtypeStruct((4 * total, 2 * 4 * total), BF16),
            jax.ShapeDtypeStruct((4 * total, 3 * 4 * total), BF16),
        ),
        [HBM] * 2,
        1000,
        [
            pltpu.VMEM((1, total), jnp.int32),
            pltpu.VMEM((4, slots, entries), BF16),
            pltpu.SemaphoreType.DMA((2,)),
        ],
    )(stay(energy_order.reshape(1, total)), stay(green_window.reshape(4, slots, entries)))
    odd = lax.axis_index("rows") % 2 == 1
    packed, first, second, odd = lax.optimization_barrier((packed, first, second, odd))
    spread = lax.all_to_all(
        packed, "energy", split_axis=0, concat_axis=0, tiled=True, axis_index_groups=[order]
    )
    sigma = call(
        convolve_kernel,
        jax.ShapeDtypeStruct((2, 4 * total, columns), BF16),
        [VMEM] * 4,
        2 * 5 * 16 * total * total * columns,
    )(first, second, spread, screened.reshape(4 * total, columns))

    groups = [
        [energy * rows + (low + side) % rows for side in range(2) for energy in order]
        for low in range(1, rows, 2)
    ]
    both = lax.all_to_all(
        sigma.reshape(2 * devices, 4 * slots, columns),
        ("energy", "rows"),
        split_axis=0,
        concat_axis=0,
        tiled=True,
        axis_index_groups=groups,
    ).reshape(2, 4 * total, columns)
    own = jnp.where(odd, both[0], both[1])
    pairs = [(row, row ^ 1) for row in range(rows)]
    near = lax.ppermute(own, "rows", pairs)

    blocks = retarded.reshape(2, slots, 3, slab, width)
    wide = (pl.cdiv(columns + padded - slab, 128), 4 * total, 128)
    out = jax.ShapeDtypeStruct((4 * slots, 1, width), F32)
    work = 2 * 8 * slots * 2 * slab * slab * width
    density = call(
        functools.partial(density_kernel, order, rows, padded),
        out,
        [SMEM] + [VMEM] * 2,
        2 * work,
        [pltpu.VMEM((2, *wide), F32)],
    )(window_start, both, blocks)
    density = call(
        functools.partial(density_near_kernel, order, padded),
        out,
        [VMEM] * 3,
        work,
        [pltpu.VMEM(wide, F32)],
    )(near, blocks, density)
    return density.reshape(2, 2, slots, 1, width)


def solution(mesh):
    in_specs = (
        P(None, None, "energy", "rows", None),
        P(None, None, None, "rows", "energy"),
        P(None, "energy", "rows", None, None, None),
        P(),
        P("rows"),
    )
    out_specs = P(None, None, "energy", "rows", None)
    return jax.shard_map(shards, mesh=mesh, in_specs=in_specs, out_specs=out_specs, check_vma=False)
```

```python
import functools
import math

import jax
import jax.numpy as jnp
from jax import lax
from jax.experimental import pallas as pl
from jax.experimental.pallas import tpu as pltpu
from jax.sharding import PartitionSpec as P

F32 = jnp.float32
BF16 = jnp.bfloat16
VMEM = pl.BlockSpec(memory_space=pltpu.VMEM)
SMEM = pl.BlockSpec(memory_space=pltpu.SMEM)
HBM = pl.BlockSpec(memory_space=pltpu.HBM)


def call(kernel, out_shape, in_specs, flops, scratch=(), moved=2**20):
    return pl.pallas_call(
        kernel,
        out_shape=out_shape,
        in_specs=in_specs,
        out_specs=jax.tree.map(lambda _: VMEM, out_shape),
        scratch_shapes=list(scratch),
        compiler_params=pltpu.CompilerParams(vmem_limit_bytes=16 * 2**20),
        cost_estimate=pl.CostEstimate(flops=flops, bytes_accessed=moved, transcendentals=0),
    )


def exchange_order(count):
    middle = count // 2 + 1
    return [(middle - at) % count for at in range(count)]


def split_high_low(values):
    high = values.astype(BF16)
    return high, (values - high.astype(F32)).astype(BF16)


def wrap(values, count):
    return values & (count - 1) if count & (count - 1) == 0 else values % count


def parts_of(values, count):
    return values >> (count.bit_length() - 1) if count & (count - 1) == 0 else values // count


def phases(energy, time, quarter, count):
    turns = wrap(4 * energy * time + count * quarter, 4 * count)
    half = jnp.where(turns >= 2 * count, turns - 2 * count, turns)
    odd = half >= count
    angle = jnp.where(odd, half - count, half).astype(F32) * (0.5 * math.pi / count)
    square = angle * angle
    cosine, sine = 0.0, 0.0
    for power in range(7, -1, -1):
        cosine = cosine * square + (-1) ** power / math.factorial(2 * power)
        sine = sine * square + (-1) ** power / math.factorial(2 * power + 1)
    value = jnp.where(odd, -sine * angle, cosine)
    return jnp.where(turns >= 2 * count, -value, value)


def tables(energy_order, order):
    total = energy_order.shape[1]
    slots = total // len(order)
    size = 4 * total
    row = lax.broadcasted_iota(jnp.int32, (size, 1), 0)
    col = lax.broadcasted_iota(jnp.int32, (1, size), 1)

    def device_at(place, places):
        found = jnp.zeros_like(place)
        for at, device in enumerate(places):
            found = jnp.where(place == at, device, found)
        return found

    across = lax.broadcasted_iota(jnp.int32, (total, total), 1)
    down = lax.broadcasted_iota(jnp.int32, (total, total), 0)
    energy_down = jnp.sum(jnp.where(across == down, energy_order, 0), axis=1, keepdims=True)

    source = device_at(parts_of(col, 4 * slots), order) * slots + wrap(col, slots)
    energy = jnp.sum(
        jnp.where(lax.broadcasted_iota(jnp.int32, (total, size), 0) == source, energy_down, 0), axis=0, keepdims=True
    )
    same = parts_of(row, 2 * total) == wrap(parts_of(col, 2 * slots), 2)
    quarter = wrap(parts_of(row, total), 2) - wrap(parts_of(col, slots), 2)
    first = jnp.where(same, phases(energy, wrap(row, total), quarter, total), 0.0)
    source = device_at(parts_of(row, 4 * slots), order) * slots + wrap(parts_of(row, 4), slots)
    energy = jnp.sum(
        jnp.where(lax.broadcasted_iota(jnp.int32, (size, total), 1) == source, energy_order, 0), axis=1, keepdims=True
    )
    same = wrap(parts_of(row, 2), 2) == parts_of(col, 2 * total)
    quarter = 1 - wrap(row, 2) + wrap(parts_of(col, total), 2)
    second = jnp.where(same, phases(energy, wrap(col, total), quarter, total), 0.0) * (1.0 / total)
    return first, second


def row_positions(slab, devices, shape):
    at = lax.broadcasted_iota(jnp.int32, shape, 0)
    return wrap(at, devices) * (slab // devices) + parts_of(at, devices)


def to_tiles(tiles_ref, values, start=0):
    rows, lanes = values.shape
    for tile in range(tiles_ref.shape[0]):
        last = min(lanes, 128 * (tile + 1))
        tiles_ref[tile, pl.ds(start, rows), : last - 128 * tile] = values[:, 128 * tile : last]


def strided_rows(tiles_ref, start, count, stride, lanes):
    found = [tiles_ref[tile, pl.ds(start, count, stride=stride), :] for tile in range(tiles_ref.shape[0])]
    return jnp.concatenate(found, axis=1)[:, :lanes]


def front_kernel(
    order,
    energy_hbm,
    green_hbm,
    out_ref,
    first_ref,
    second_ref,
    energy_ref,
    green_ref,
    sems,
):
    pairs = ((energy_hbm, energy_ref), (green_hbm, green_ref))
    copies = [pltpu.make_async_copy(source, target, sems.at[at]) for at, (source, target) in enumerate(pairs)]
    for copy in copies:
        copy.start()
    copies[0].wait()
    first, second = tables(energy_ref[...], order)
    first_high, first_low = split_high_low(first)
    second_high, second_low = split_high_low(second)
    first_ref[...] = jnp.concatenate([first_high, first_low], axis=1)
    second_ref[...] = jnp.concatenate([second_high, second_low, second_high], axis=1)
    copies[1].wait()
    pairs, slots, entries = green_ref.shape
    columns = entries // len(order)
    whole = jnp.concatenate([green_ref[at].astype(F32) for at in range(pairs)], axis=0)
    parts = [whole[:, device * columns : (device + 1) * columns] for device in order]
    out_ref[...] = jnp.concatenate(parts, axis=0).astype(BF16)


def convolve_kernel(first_ref, second_ref, spread_ref, screen_ref, out_ref):
    total = screen_ref.shape[0] // 4
    spread = spread_ref[...]
    times = jnp.dot(first_ref[...], jnp.concatenate([spread, spread], axis=0), preferred_element_type=F32)
    screen = screen_ref[...].astype(F32)
    mixed = []
    for kind in range(2):
        base = kind * 2 * total
        times_re, times_im = times[base : base + total], times[base + total : base + 2 * total]
        screen_re, screen_im = screen[base : base + total], screen[base + total : base + 2 * total]
        mixed.append(times_re * screen_re - times_im * screen_im)
        mixed.append(times_re * screen_im + times_im * screen_re)
    mixed_high, mixed_low = split_high_low(jnp.concatenate(mixed, axis=0))
    sigma = jnp.dot(
        second_ref[...],
        jnp.concatenate([mixed_high, mixed_high, mixed_low], axis=0),
        preferred_element_type=F32,
    ).astype(BF16)
    out_ref[0] = sigma
    out_ref[1] = sigma


def spread_rows(sigma_ref, wide_ref, slab, padded, places):
    devices = len(places)
    each = sigma_ref.shape[0] // devices
    depth = slab // devices
    wide = sigma_ref[...].astype(F32)
    lanes = wide_ref.shape[0] * 128
    wide = jnp.concatenate([wide, jnp.zeros((wide.shape[0], lanes - wide.shape[1]), F32)], axis=1)
    for at, device in enumerate(places):
        to_tiles(wide_ref, wide[at * each : (at + 1) * each], device * each)
    matrices = []
    for at in range(each):
        flat = strided_rows(wide_ref, at, devices, each, lanes)
        matrices.append(
            jnp.concatenate([flat[:, slab * i : slab * i + padded] for i in range(depth)], axis=0)
        )
    return matrices


def row_order(slab, devices):
    shape = (slab, slab)
    return jnp.where(
        row_positions(slab, devices, shape) == lax.broadcasted_iota(jnp.int32, shape, 1), 1.0, 0.0
    ).astype(BF16)


def neighbour_density(matrices, blocks_ref, slot, block, ordering):
    real, imag = blocks_ref[0, slot, block], blocks_ref[1, slot, block]
    slab, width = real.shape
    gap = jnp.zeros((matrices[0].shape[1] - slab, width), BF16)
    left = jnp.concatenate(
        [
            jnp.concatenate([matrices[slot * 4 + kind * 2], matrices[slot * 4 + kind * 2 + 1]], axis=1)
            for kind in range(2)
        ],
        axis=0,
    ).astype(BF16)
    inner_re = jnp.dot(left, jnp.concatenate([real, gap, imag, gap], axis=0), preferred_element_type=F32)
    inner_im = jnp.dot(left, jnp.concatenate([-imag, gap, real, gap], axis=0), preferred_element_type=F32)
    wide_re = jnp.dot(ordering, real, preferred_element_type=F32)
    wide_im = jnp.dot(ordering, imag, preferred_element_type=F32)
    result = []
    for kind in range(2):
        z_re = inner_re[kind * slab : (kind + 1) * slab]
        z_im = inner_im[kind * slab : (kind + 1) * slab]
        result.append((z_re * wide_re - z_im * wide_im, z_re * wide_im + z_im * wide_re))
    return result


def density_kernel(order, rows, padded, start_ref, sigma_ref, blocks_ref, out_ref, wide_ref):
    slots, _, slab, width = blocks_ref.shape[1:]
    devices = len(order)
    row = lax.axis_index("rows")
    odd = lax.rem(row, 2)
    has_far = jnp.where(jnp.logical_and(row > 0, row < rows - 1), 1.0, 0.0)
    own = spread_rows(sigma_ref.at[1 - odd], wide_ref.at[0], slab, padded, order)
    far = spread_rows(sigma_ref.at[odd], wide_ref.at[1], slab, padded, order)
    on_diagonal = row_positions(slab, devices, (slab, padded)) == lax.broadcasted_iota(jnp.int32, (slab, padded), 1)
    diagonal = jnp.concatenate(
        [jnp.sum(jnp.where(on_diagonal, matrix, 0.0), axis=0, keepdims=True) for matrix in own], axis=0
    )
    at_row = lax.broadcasted_iota(jnp.int32, (padded, width), 0)
    placed = at_row + start_ref[0] == lax.broadcasted_iota(jnp.int32, (padded, width), 1)
    place = jnp.where(jnp.logical_and(placed, at_row < slab), 1.0, 0.0).astype(BF16)
    direct = jnp.dot(diagonal.astype(BF16), place, preferred_element_type=F32)
    ordering = row_order(slab, devices)
    for slot in range(slots):
        here = neighbour_density(own, blocks_ref, slot, 1, ordering)
        there = neighbour_density(far, blocks_ref, slot, 2 * odd, ordering)
        for kind in range(2):
            for part in range(2):
                at = slot * 4 + kind * 2 + part
                out_ref[(kind * 2 + part) * slots + slot] = direct[at : at + 1] + jnp.sum(
                    here[kind][part] + there[kind][part] * has_far, axis=0, keepdims=True
                )


def density_near_kernel(order, padded, sigma_ref, blocks_ref, before_ref, out_ref, wide_ref):
    slots, _, slab, _ = blocks_ref.shape[1:]
    near = spread_rows(sigma_ref, wide_ref, slab, padded, order)
    ordering = row_order(slab, len(order))
    block = 2 - 2 * lax.rem(lax.axis_index("rows"), 2)
    for slot in range(slots):
        found = neighbour_density(near, blocks_ref, slot, block, ordering)
        for kind in range(2):
            for part in range(2):
                at = (kind * 2 + part) * slots + slot
                out_ref[at] = before_ref[at] + jnp.sum(found[kind][part], axis=0, keepdims=True)


def shards(green_window, screened, retarded, energy_order, window_start):
    devices = lax.axis_size("energy")
    rows = lax.axis_size("rows")
    slots, entries = green_window.shape[2], green_window.shape[4]
    slab, width = retarded.shape[4], retarded.shape[5]
    total = devices * slots
    columns = entries // devices
    order = exchange_order(devices)
    padded = pl.cdiv(slab, 128) * 128

    def stay(values):
        return pltpu.with_memory_space_constraint(values, pltpu.HBM)

    packed, first, second = call(
        functools.partial(front_kernel, order),
        (
            jax.ShapeDtypeStruct((4 * total, columns), BF16),
            jax.ShapeDtypeStruct((4 * total, 2 * 4 * total), BF16),
            jax.ShapeDtypeStruct((4 * total, 3 * 4 * total), BF16),
        ),
        [HBM] * 2,
        1000,
        [
            pltpu.VMEM((1, total), jnp.int32),
            pltpu.VMEM((4, slots, entries), BF16),
            pltpu.SemaphoreType.DMA((2,)),
        ],
    )(stay(energy_order.reshape(1, total)), stay(green_window.reshape(4, slots, entries)))
    odd = lax.axis_index("rows") % 2 == 1
    packed, first, second, odd = lax.optimization_barrier((packed, first, second, odd))
    spread = lax.all_to_all(
        packed, "energy", split_axis=0, concat_axis=0, tiled=True, axis_index_groups=[order]
    )
    sigma = call(
        convolve_kernel,
        jax.ShapeDtypeStruct((2, 4 * total, columns), BF16),
        [VMEM] * 4,
        2 * 5 * 16 * total * total * columns,
    )(first, second, spread, screened.reshape(4 * total, columns))

    groups = [
        [energy * rows + (low + side) % rows for side in range(2) for energy in order]
        for low in range(1, rows, 2)
    ]
    both = lax.all_to_all(
        sigma.reshape(2 * devices, 4 * slots, columns),
        ("energy", "rows"),
        split_axis=0,
        concat_axis=0,
        tiled=True,
        axis_index_groups=groups,
    ).reshape(2, 4 * total, columns)
    own = jnp.where(odd, both[0], both[1])
    pairs = [(row, row ^ 1) for row in range(rows)]
    near = lax.ppermute(own, "rows", pairs)

    blocks = retarded.reshape(2, slots, 3, slab, width)
    wide = (pl.cdiv(columns + padded - slab, 128), 4 * total, 128)
    out = jax.ShapeDtypeStruct((4 * slots, 1, width), F32)
    work = 2 * 8 * slots * 2 * slab * slab * width
    density = call(
        functools.partial(density_kernel, order, rows, padded),
        out,
        [SMEM] + [VMEM] * 2,
        2 * work,
        [pltpu.VMEM((2, *wide), F32)],
    )(window_start, both, blocks)
    density = call(
        functools.partial(density_near_kernel, order, padded),
        out,
        [VMEM] * 3,
        work,
        [pltpu.VMEM(wide, F32)],
    )(near, blocks, density)
    return density.reshape(2, 2, slots, 1, width)


def solution(mesh):
    in_specs = (
        P(None, None, "energy", "rows", None),
        P(None, None, None, "rows", "energy"),
        P(None, "energy", "rows", None, None, None),
        P(),
        P("rows"),
    )
    out_specs = P(None, None, "energy", "rows", None)
    return jax.shard_map(shards, mesh=mesh, in_specs=in_specs, out_specs=out_specs, check_vma=False)
```

```python
import functools
import math

import jax
import jax.numpy as jnp
from jax import lax
from jax.experimental import pallas as pl
from jax.experimental.pallas import tpu as pltpu
from jax.sharding import PartitionSpec as P

F32 = jnp.float32
BF16 = jnp.bfloat16
VMEM = pl.BlockSpec(memory_space=pltpu.VMEM)
SMEM = pl.BlockSpec(memory_space=pltpu.SMEM)


def call(kernel, out_shape, in_specs, flops, scratch=(), moved=2**20):
    return pl.pallas_call(
        kernel,
        out_shape=out_shape,
        in_specs=in_specs,
        out_specs=jax.tree.map(lambda _: VMEM, out_shape),
        scratch_shapes=list(scratch),
        compiler_params=pltpu.CompilerParams(vmem_limit_bytes=16 * 2**20),
        cost_estimate=pl.CostEstimate(flops=flops, bytes_accessed=moved, transcendentals=0),
    )


def exchange_order(count):
    middle = count // 2 + 1
    return [(middle - at) % count for at in range(count)]


def split_high_low(values):
    high = values.astype(BF16)
    return high, (values - high.astype(F32)).astype(BF16)


def wrap(values, count):
    return values & (count - 1) if count & (count - 1) == 0 else values % count


def parts_of(values, count):
    return values >> (count.bit_length() - 1) if count & (count - 1) == 0 else values // count


def phases(energy, time, quarter, count):
    turns = wrap(4 * energy * time + count * quarter, 4 * count)
    half = jnp.where(turns >= 2 * count, turns - 2 * count, turns)
    odd = half >= count
    angle = jnp.where(odd, half - count, half).astype(F32) * (0.5 * math.pi / count)
    square = angle * angle
    cosine, sine = 0.0, 0.0
    for power in range(7, -1, -1):
        cosine = cosine * square + (-1) ** power / math.factorial(2 * power)
        sine = sine * square + (-1) ** power / math.factorial(2 * power + 1)
    value = jnp.where(odd, -sine * angle, cosine)
    return jnp.where(turns >= 2 * count, -value, value)


def tables(energy_order, order):
    total = energy_order.shape[1]
    slots = total // len(order)
    size = 4 * total
    row = lax.broadcasted_iota(jnp.int32, (size, 1), 0)
    col = lax.broadcasted_iota(jnp.int32, (1, size), 1)

    def device_at(place, places):
        found = jnp.zeros_like(place)
        for at, device in enumerate(places):
            found = jnp.where(place == at, device, found)
        return found

    across = lax.broadcasted_iota(jnp.int32, (total, total), 1)
    down = lax.broadcasted_iota(jnp.int32, (total, total), 0)
    energy_down = jnp.sum(jnp.where(across == down, energy_order, 0), axis=1, keepdims=True)

    source = device_at(parts_of(col, 4 * slots), order) * slots + wrap(col, slots)
    energy = jnp.sum(
        jnp.where(lax.broadcasted_iota(jnp.int32, (total, size), 0) == source, energy_down, 0), axis=0, keepdims=True
    )
    same = parts_of(row, 2 * total) == wrap(parts_of(col, 2 * slots), 2)
    quarter = wrap(parts_of(row, total), 2) - wrap(parts_of(col, slots), 2)
    first = jnp.where(same, phases(energy, wrap(row, total), quarter, total), 0.0)
    source = device_at(parts_of(row, 4 * slots), order) * slots + wrap(parts_of(row, 4), slots)
    energy = jnp.sum(
        jnp.where(lax.broadcasted_iota(jnp.int32, (size, total), 1) == source, energy_order, 0), axis=1, keepdims=True
    )
    same = wrap(parts_of(row, 2), 2) == parts_of(col, 2 * total)
    quarter = 1 - wrap(row, 2) + wrap(parts_of(col, total), 2)
    second = jnp.where(same, phases(energy, wrap(col, total), quarter, total), 0.0) * (1.0 / total)
    return first, second


def row_positions(slab, devices, shape):
    at = lax.broadcasted_iota(jnp.int32, shape, 0)
    return wrap(at, devices) * (slab // devices) + parts_of(at, devices)


def to_tiles(tiles_ref, values, start=0):
    rows, lanes = values.shape
    for tile in range(tiles_ref.shape[0]):
        last = min(lanes, 128 * (tile + 1))
        tiles_ref[tile, pl.ds(start, rows), : last - 128 * tile] = values[:, 128 * tile : last]


def strided_rows(tiles_ref, start, count, stride, lanes):
    found = [tiles_ref[tile, pl.ds(start, count, stride=stride), :] for tile in range(tiles_ref.shape[0])]
    return jnp.concatenate(found, axis=1)[:, :lanes]


def pack_kernel(order, green_ref, out_ref):
    pairs, slots, entries = green_ref.shape
    columns = entries // len(order)
    whole = jnp.concatenate([green_ref[at].astype(F32) for at in range(pairs)], axis=0)
    parts = [whole[:, device * columns : (device + 1) * columns] for device in order]
    out_ref[...] = jnp.concatenate(parts, axis=0).astype(BF16)


def tables_kernel(order, energy_ref, first_ref, second_ref):
    first, second = tables(energy_ref[...], order)
    first_high, first_low = split_high_low(first)
    second_high, second_low = split_high_low(second)
    first_ref[...] = jnp.concatenate([first_high, first_low], axis=1)
    second_ref[...] = jnp.concatenate([second_high, second_low, second_high], axis=1)


def convolve_kernel(first_ref, second_ref, spread_ref, screen_ref, out_ref):
    total = screen_ref.shape[0] // 4
    spread = spread_ref[...]
    times = jnp.dot(first_ref[...], jnp.concatenate([spread, spread], axis=0), preferred_element_type=F32)
    screen = screen_ref[...].astype(F32)
    mixed = []
    for kind in range(2):
        base = kind * 2 * total
        times_re, times_im = times[base : base + total], times[base + total : base + 2 * total]
        screen_re, screen_im = screen[base : base + total], screen[base + total : base + 2 * total]
        mixed.append(times_re * screen_re - times_im * screen_im)
        mixed.append(times_re * screen_im + times_im * screen_re)
    mixed_high, mixed_low = split_high_low(jnp.concatenate(mixed, axis=0))
    sigma = jnp.dot(
        second_ref[...],
        jnp.concatenate([mixed_high, mixed_high, mixed_low], axis=0),
        preferred_element_type=F32,
    ).astype(BF16)
    out_ref[0] = sigma
    out_ref[1] = sigma


def spread_rows(sigma_ref, wide_ref, slab, padded, places):
    devices = len(places)
    each = sigma_ref.shape[0] // devices
    depth = slab // devices
    wide = sigma_ref[...].astype(F32)
    lanes = wide_ref.shape[0] * 128
    wide = jnp.concatenate([wide, jnp.zeros((wide.shape[0], lanes - wide.shape[1]), F32)], axis=1)
    for at, device in enumerate(places):
        to_tiles(wide_ref, wide[at * each : (at + 1) * each], device * each)
    matrices = []
    for at in range(each):
        flat = strided_rows(wide_ref, at, devices, each, lanes)
        matrices.append(
            jnp.concatenate([flat[:, slab * i : slab * i + padded] for i in range(depth)], axis=0)
        )
    return matrices


def row_order(slab, devices):
    shape = (slab, slab)
    return jnp.where(
        row_positions(slab, devices, shape) == lax.broadcasted_iota(jnp.int32, shape, 1), 1.0, 0.0
    ).astype(BF16)


def neighbour_density(matrices, blocks_ref, slot, block, ordering):
    real, imag = blocks_ref[0, slot, block], blocks_ref[1, slot, block]
    slab, width = real.shape
    gap = jnp.zeros((matrices[0].shape[1] - slab, width), BF16)
    left = jnp.concatenate(
        [
            jnp.concatenate([matrices[slot * 4 + kind * 2], matrices[slot * 4 + kind * 2 + 1]], axis=1)
            for kind in range(2)
        ],
        axis=0,
    ).astype(BF16)
    inner_re = jnp.dot(left, jnp.concatenate([real, gap, imag, gap], axis=0), preferred_element_type=F32)
    inner_im = jnp.dot(left, jnp.concatenate([-imag, gap, real, gap], axis=0), preferred_element_type=F32)
    wide_re = jnp.dot(ordering, real, preferred_element_type=F32)
    wide_im = jnp.dot(ordering, imag, preferred_element_type=F32)
    result = []
    for kind in range(2):
        z_re = inner_re[kind * slab : (kind + 1) * slab]
        z_im = inner_im[kind * slab : (kind + 1) * slab]
        result.append((z_re * wide_re - z_im * wide_im, z_re * wide_im + z_im * wide_re))
    return result


def density_kernel(order, rows, padded, start_ref, sigma_ref, blocks_ref, out_ref, wide_ref):
    slots, _, slab, width = blocks_ref.shape[1:]
    devices = len(order)
    row = lax.axis_index("rows")
    odd = lax.rem(row, 2)
    has_far = jnp.where(jnp.logical_and(row > 0, row < rows - 1), 1.0, 0.0)
    own = spread_rows(sigma_ref.at[1 - odd], wide_ref.at[0], slab, padded, order)
    far = spread_rows(sigma_ref.at[odd], wide_ref.at[1], slab, padded, order)
    on_diagonal = row_positions(slab, devices, (slab, padded)) == lax.broadcasted_iota(jnp.int32, (slab, padded), 1)
    diagonal = jnp.concatenate(
        [jnp.sum(jnp.where(on_diagonal, matrix, 0.0), axis=0, keepdims=True) for matrix in own], axis=0
    )
    at_row = lax.broadcasted_iota(jnp.int32, (padded, width), 0)
    placed = at_row + start_ref[0] == lax.broadcasted_iota(jnp.int32, (padded, width), 1)
    place = jnp.where(jnp.logical_and(placed, at_row < slab), 1.0, 0.0).astype(BF16)
    direct = jnp.dot(diagonal.astype(BF16), place, preferred_element_type=F32)
    ordering = row_order(slab, devices)
    for slot in range(slots):
        here = neighbour_density(own, blocks_ref, slot, 1, ordering)
        there = neighbour_density(far, blocks_ref, slot, 2 * odd, ordering)
        for kind in range(2):
            for part in range(2):
                at = slot * 4 + kind * 2 + part
                out_ref[(kind * 2 + part) * slots + slot] = direct[at : at + 1] + jnp.sum(
                    here[kind][part] + there[kind][part] * has_far, axis=0, keepdims=True
                )


def density_near_kernel(order, padded, sigma_ref, blocks_ref, before_ref, out_ref, wide_ref):
    slots, _, slab, _ = blocks_ref.shape[1:]
    near = spread_rows(sigma_ref, wide_ref, slab, padded, order)
    ordering = row_order(slab, len(order))
    block = 2 - 2 * lax.rem(lax.axis_index("rows"), 2)
    for slot in range(slots):
        found = neighbour_density(near, blocks_ref, slot, block, ordering)
        for kind in range(2):
            for part in range(2):
                at = (kind * 2 + part) * slots + slot
                out_ref[at] = before_ref[at] + jnp.sum(found[kind][part], axis=0, keepdims=True)


def shards(green_window, screened, retarded, energy_order, window_start):
    devices = lax.axis_size("energy")
    rows = lax.axis_size("rows")
    slots, entries = green_window.shape[2], green_window.shape[4]
    slab, width = retarded.shape[4], retarded.shape[5]
    total = devices * slots
    columns = entries // devices
    order = exchange_order(devices)
    padded = pl.cdiv(slab, 128) * 128

    packed = call(
        functools.partial(pack_kernel, order), jax.ShapeDtypeStruct((4 * total, columns), BF16), [VMEM], 1000
    )(green_window.reshape(4, slots, entries))
    first, second = call(
        functools.partial(tables_kernel, order),
        (
            jax.ShapeDtypeStruct((4 * total, 2 * 4 * total), BF16),
            jax.ShapeDtypeStruct((4 * total, 3 * 4 * total), BF16),
        ),
        [VMEM],
        1000,
    )(energy_order.reshape(1, total))
    spread = lax.all_to_all(
        packed, "energy", split_axis=0, concat_axis=0, tiled=True, axis_index_groups=[order]
    )
    odd = lax.axis_index("rows") % 2 == 1
    spread, first, second, odd = lax.optimization_barrier((spread, first, second, odd))
    sigma = call(
        convolve_kernel,
        jax.ShapeDtypeStruct((2, 4 * total, columns), BF16),
        [VMEM] * 4,
        2 * 5 * 16 * total * total * columns,
    )(first, second, spread, screened.reshape(4 * total, columns))

    groups = [
        [energy * rows + (low + side) % rows for side in range(2) for energy in order]
        for low in range(1, rows, 2)
    ]
    both = lax.all_to_all(
        sigma.reshape(2 * devices, 4 * slots, columns),
        ("energy", "rows"),
        split_axis=0,
        concat_axis=0,
        tiled=True,
        axis_index_groups=groups,
    ).reshape(2, 4 * total, columns)
    own = jnp.where(odd, both[0], both[1])
    pairs = [(row, row ^ 1) for row in range(rows)]
    near = lax.ppermute(own, "rows", pairs)

    blocks = retarded.reshape(2, slots, 3, slab, width)
    wide = (pl.cdiv(columns + padded - slab, 128), 4 * total, 128)
    out = jax.ShapeDtypeStruct((4 * slots, 1, width), F32)
    work = 2 * 8 * slots * 2 * slab * slab * width
    density = call(
        functools.partial(density_kernel, order, rows, padded),
        out,
        [SMEM] + [VMEM] * 2,
        2 * work,
        [pltpu.VMEM((2, *wide), F32)],
    )(window_start, both, blocks)
    density = call(
        functools.partial(density_near_kernel, order, padded),
        out,
        [VMEM] * 3,
        work,
        [pltpu.VMEM(wide, F32)],
    )(near, blocks, density)
    return density.reshape(2, 2, slots, 1, width)


def solution(mesh):
    in_specs = (
        P(None, None, "energy", "rows", None),
        P(None, None, None, "rows", "energy"),
        P(None, "energy", "rows", None, None, None),
        P(),
        P("rows"),
    )
    out_specs = P(None, None, "energy", "rows", None)
    return jax.shard_map(shards, mesh=mesh, in_specs=in_specs, out_specs=out_specs, check_vma=False)
```

```python
import functools
import math

import jax
import jax.numpy as jnp
from jax import lax
from jax.experimental import pallas as pl
from jax.experimental.pallas import tpu as pltpu
from jax.sharding import PartitionSpec as P

F32 = jnp.float32
BF16 = jnp.bfloat16
VMEM = pl.BlockSpec(memory_space=pltpu.VMEM)
SMEM = pl.BlockSpec(memory_space=pltpu.SMEM)
HBM = pl.BlockSpec(memory_space=pltpu.HBM)


def call(kernel, out_shape, in_specs, flops, scratch=(), moved=2**20):
    return pl.pallas_call(
        kernel,
        out_shape=out_shape,
        in_specs=in_specs,
        out_specs=jax.tree.map(lambda _: VMEM, out_shape),
        scratch_shapes=list(scratch),
        compiler_params=pltpu.CompilerParams(vmem_limit_bytes=16 * 2**20),
        cost_estimate=pl.CostEstimate(flops=flops, bytes_accessed=moved, transcendentals=0),
    )


def exchange_order(count):
    middle = count // 2 + 1
    step = 3 if math.gcd(3, count) == 1 else 1
    return [(middle + step * at) % count for at in range(count)]


def split_high_low(values):
    high = values.astype(BF16)
    return high, (values - high.astype(F32)).astype(BF16)


def wrap(values, count):
    return values & (count - 1) if count & (count - 1) == 0 else values % count


def parts_of(values, count):
    return values >> (count.bit_length() - 1) if count & (count - 1) == 0 else values // count


def phases(energy, time, quarter, count):
    turns = wrap(4 * energy * time + count * quarter, 4 * count)
    half = jnp.where(turns >= 2 * count, turns - 2 * count, turns)
    odd = half >= count
    angle = jnp.where(odd, half - count, half).astype(F32) * (0.5 * math.pi / count)
    square = angle * angle
    cosine, sine = 0.0, 0.0
    for power in range(7, -1, -1):
        cosine = cosine * square + (-1) ** power / math.factorial(2 * power)
        sine = sine * square + (-1) ** power / math.factorial(2 * power + 1)
    value = jnp.where(odd, -sine * angle, cosine)
    return jnp.where(turns >= 2 * count, -value, value)


def tables(energy_order, order):
    total = energy_order.shape[1]
    slots = total // len(order)
    size = 4 * total
    row = lax.broadcasted_iota(jnp.int32, (size, 1), 0)
    col = lax.broadcasted_iota(jnp.int32, (1, size), 1)

    def device_at(place, places):
        found = jnp.zeros_like(place)
        for at, device in enumerate(places):
            found = jnp.where(place == at, device, found)
        return found

    across = lax.broadcasted_iota(jnp.int32, (total, total), 1)
    down = lax.broadcasted_iota(jnp.int32, (total, total), 0)
    energy_down = jnp.sum(jnp.where(across == down, energy_order, 0), axis=1, keepdims=True)

    source = device_at(parts_of(col, 4 * slots), order) * slots + wrap(col, slots)
    energy = jnp.sum(
        jnp.where(lax.broadcasted_iota(jnp.int32, (total, size), 0) == source, energy_down, 0), axis=0, keepdims=True
    )
    same = parts_of(row, 2 * total) == wrap(parts_of(col, 2 * slots), 2)
    quarter = wrap(parts_of(row, total), 2) - wrap(parts_of(col, slots), 2)
    first = jnp.where(same, phases(energy, wrap(row, total), quarter, total), 0.0)
    source = device_at(parts_of(row, 4 * slots), order) * slots + wrap(parts_of(row, 4), slots)
    energy = jnp.sum(
        jnp.where(lax.broadcasted_iota(jnp.int32, (size, total), 1) == source, energy_order, 0), axis=1, keepdims=True
    )
    same = wrap(parts_of(row, 2), 2) == parts_of(col, 2 * total)
    quarter = 1 - wrap(row, 2) + wrap(parts_of(col, total), 2)
    second = jnp.where(same, phases(energy, wrap(col, total), quarter, total), 0.0) * (1.0 / total)
    return first, second


def row_positions(slab, devices, shape):
    at = lax.broadcasted_iota(jnp.int32, shape, 0)
    return wrap(at, devices) * (slab // devices) + parts_of(at, devices)


def to_tiles(tiles_ref, values, start=0):
    rows, lanes = values.shape
    for tile in range(tiles_ref.shape[0]):
        last = min(lanes, 128 * (tile + 1))
        tiles_ref[tile, pl.ds(start, rows), : last - 128 * tile] = values[:, 128 * tile : last]


def strided_rows(tiles_ref, start, count, stride, lanes):
    found = [tiles_ref[tile, pl.ds(start, count, stride=stride), :] for tile in range(tiles_ref.shape[0])]
    return jnp.concatenate(found, axis=1)[:, :lanes]


def front_kernel(
    order,
    energy_hbm,
    green_hbm,
    out_ref,
    first_ref,
    second_ref,
    energy_ref,
    green_ref,
    sems,
):
    pairs = ((energy_hbm, energy_ref), (green_hbm, green_ref))
    copies = [pltpu.make_async_copy(source, target, sems.at[at]) for at, (source, target) in enumerate(pairs)]
    for copy in copies:
        copy.start()
    copies[0].wait()
    first, second = tables(energy_ref[...], order)
    first_high, first_low = split_high_low(first)
    second_high, second_low = split_high_low(second)
    first_ref[...] = jnp.concatenate([first_high, first_low], axis=1)
    second_ref[...] = jnp.concatenate([second_high, second_low, second_high], axis=1)
    copies[1].wait()
    pairs, slots, entries = green_ref.shape
    columns = entries // len(order)
    whole = jnp.concatenate([green_ref[at].astype(F32) for at in range(pairs)], axis=0)
    parts = [whole[:, device * columns : (device + 1) * columns] for device in order]
    out_ref[...] = jnp.concatenate(parts, axis=0).astype(BF16)


def convolve_kernel(first_ref, second_ref, spread_ref, screen_ref, out_ref):
    total = screen_ref.shape[0] // 4
    spread = spread_ref[...]
    times = jnp.dot(first_ref[...], jnp.concatenate([spread, spread], axis=0), preferred_element_type=F32)
    screen = screen_ref[...].astype(F32)
    mixed = []
    for kind in range(2):
        base = kind * 2 * total
        times_re, times_im = times[base : base + total], times[base + total : base + 2 * total]
        screen_re, screen_im = screen[base : base + total], screen[base + total : base + 2 * total]
        mixed.append(times_re * screen_re - times_im * screen_im)
        mixed.append(times_re * screen_im + times_im * screen_re)
    mixed_high, mixed_low = split_high_low(jnp.concatenate(mixed, axis=0))
    sigma = jnp.dot(
        second_ref[...],
        jnp.concatenate([mixed_high, mixed_high, mixed_low], axis=0),
        preferred_element_type=F32,
    ).astype(BF16)
    out_ref[0] = sigma
    out_ref[1] = sigma


def spread_rows(sigma_ref, wide_ref, slab, padded, places):
    devices = len(places)
    each = sigma_ref.shape[0] // devices
    depth = slab // devices
    wide = sigma_ref[...].astype(F32)
    lanes = wide_ref.shape[0] * 128
    wide = jnp.concatenate([wide, jnp.zeros((wide.shape[0], lanes - wide.shape[1]), F32)], axis=1)
    for at, device in enumerate(places):
        to_tiles(wide_ref, wide[at * each : (at + 1) * each], device * each)
    matrices = []
    for at in range(each):
        flat = strided_rows(wide_ref, at, devices, each, lanes)
        matrices.append(
            jnp.concatenate([flat[:, slab * i : slab * i + padded] for i in range(depth)], axis=0)
        )
    return matrices


def row_order(slab, devices):
    shape = (slab, slab)
    return jnp.where(
        row_positions(slab, devices, shape) == lax.broadcasted_iota(jnp.int32, shape, 1), 1.0, 0.0
    ).astype(BF16)


def neighbour_density(matrices, blocks_ref, slot, block, ordering):
    real, imag = blocks_ref[0, slot, block], blocks_ref[1, slot, block]
    slab, width = real.shape
    gap = jnp.zeros((matrices[0].shape[1] - slab, width), BF16)
    left = jnp.concatenate(
        [
            jnp.concatenate([matrices[slot * 4 + kind * 2], matrices[slot * 4 + kind * 2 + 1]], axis=1)
            for kind in range(2)
        ],
        axis=0,
    ).astype(BF16)
    inner_re = jnp.dot(left, jnp.concatenate([real, gap, imag, gap], axis=0), preferred_element_type=F32)
    inner_im = jnp.dot(left, jnp.concatenate([-imag, gap, real, gap], axis=0), preferred_element_type=F32)
    wide_re = jnp.dot(ordering, real, preferred_element_type=F32)
    wide_im = jnp.dot(ordering, imag, preferred_element_type=F32)
    result = []
    for kind in range(2):
        z_re = inner_re[kind * slab : (kind + 1) * slab]
        z_im = inner_im[kind * slab : (kind + 1) * slab]
        result.append((z_re * wide_re - z_im * wide_im, z_re * wide_im + z_im * wide_re))
    return result


def density_kernel(order, rows, padded, start_ref, sigma_ref, blocks_ref, out_ref, wide_ref):
    slots, _, slab, width = blocks_ref.shape[1:]
    devices = len(order)
    row = lax.axis_index("rows")
    odd = lax.rem(row, 2)
    has_far = jnp.where(jnp.logical_and(row > 0, row < rows - 1), 1.0, 0.0)
    own = spread_rows(sigma_ref.at[1 - odd], wide_ref.at[0], slab, padded, order)
    far = spread_rows(sigma_ref.at[odd], wide_ref.at[1], slab, padded, order)
    on_diagonal = row_positions(slab, devices, (slab, padded)) == lax.broadcasted_iota(jnp.int32, (slab, padded), 1)
    diagonal = jnp.concatenate(
        [jnp.sum(jnp.where(on_diagonal, matrix, 0.0), axis=0, keepdims=True) for matrix in own], axis=0
    )
    at_row = lax.broadcasted_iota(jnp.int32, (padded, width), 0)
    placed = at_row + start_ref[0] == lax.broadcasted_iota(jnp.int32, (padded, width), 1)
    place = jnp.where(jnp.logical_and(placed, at_row < slab), 1.0, 0.0).astype(BF16)
    direct = jnp.dot(diagonal.astype(BF16), place, preferred_element_type=F32)
    ordering = row_order(slab, devices)
    for slot in range(slots):
        here = neighbour_density(own, blocks_ref, slot, 1, ordering)
        there = neighbour_density(far, blocks_ref, slot, 2 * odd, ordering)
        for kind in range(2):
            for part in range(2):
                at = slot * 4 + kind * 2 + part
                out_ref[(kind * 2 + part) * slots + slot] = direct[at : at + 1] + jnp.sum(
                    here[kind][part] + there[kind][part] * has_far, axis=0, keepdims=True
                )


def density_near_kernel(order, padded, sigma_ref, blocks_ref, before_ref, out_ref, wide_ref):
    slots, _, slab, _ = blocks_ref.shape[1:]
    near = spread_rows(sigma_ref, wide_ref, slab, padded, order)
    ordering = row_order(slab, len(order))
    block = 2 - 2 * lax.rem(lax.axis_index("rows"), 2)
    for slot in range(slots):
        found = neighbour_density(near, blocks_ref, slot, block, ordering)
        for kind in range(2):
            for part in range(2):
                at = (kind * 2 + part) * slots + slot
                out_ref[at] = before_ref[at] + jnp.sum(found[kind][part], axis=0, keepdims=True)


def shards(green_window, screened, retarded, energy_order, window_start):
    devices = lax.axis_size("energy")
    rows = lax.axis_size("rows")
    slots, entries = green_window.shape[2], green_window.shape[4]
    slab, width = retarded.shape[4], retarded.shape[5]
    total = devices * slots
    columns = entries // devices
    order = exchange_order(devices)
    padded = pl.cdiv(slab, 128) * 128

    def stay(values):
        return pltpu.with_memory_space_constraint(values, pltpu.HBM)

    packed, first, second = call(
        functools.partial(front_kernel, order),
        (
            jax.ShapeDtypeStruct((4 * total, columns), BF16),
            jax.ShapeDtypeStruct((4 * total, 2 * 4 * total), BF16),
            jax.ShapeDtypeStruct((4 * total, 3 * 4 * total), BF16),
        ),
        [HBM] * 2,
        1000,
        [
            pltpu.VMEM((1, total), jnp.int32),
            pltpu.VMEM((4, slots, entries), BF16),
            pltpu.SemaphoreType.DMA((2,)),
        ],
    )(stay(energy_order.reshape(1, total)), stay(green_window.reshape(4, slots, entries)))
    odd = lax.axis_index("rows") % 2 == 1
    packed, first, second, odd = lax.optimization_barrier((packed, first, second, odd))
    spread = lax.all_to_all(
        packed, "energy", split_axis=0, concat_axis=0, tiled=True, axis_index_groups=[order]
    )
    sigma = call(
        convolve_kernel,
        jax.ShapeDtypeStruct((2, 4 * total, columns), BF16),
        [VMEM] * 4,
        2 * 5 * 16 * total * total * columns,
    )(first, second, spread, screened.reshape(4 * total, columns))

    groups = [
        [energy * rows + (low + side) % rows for side in range(2) for energy in order]
        for low in range(1, rows, 2)
    ]
    both = lax.all_to_all(
        sigma.reshape(2 * devices, 4 * slots, columns),
        ("energy", "rows"),
        split_axis=0,
        concat_axis=0,
        tiled=True,
        axis_index_groups=groups,
    ).reshape(2, 4 * total, columns)
    own = jnp.where(odd, both[0], both[1])
    pairs = [(row, row ^ 1) for row in range(rows)]
    near = lax.ppermute(own, "rows", pairs)

    blocks = retarded.reshape(2, slots, 3, slab, width)
    wide = (pl.cdiv(columns + padded - slab, 128), 4 * total, 128)
    out = jax.ShapeDtypeStruct((4 * slots, 1, width), F32)
    work = 2 * 8 * slots * 2 * slab * slab * width
    density = call(
        functools.partial(density_kernel, order, rows, padded),
        out,
        [SMEM] + [VMEM] * 2,
        2 * work,
        [pltpu.VMEM((2, *wide), F32)],
    )(window_start, both, blocks)
    density = call(
        functools.partial(density_near_kernel, order, padded),
        out,
        [VMEM] * 3,
        work,
        [pltpu.VMEM(wide, F32)],
    )(near, blocks, density)
    return density.reshape(2, 2, slots, 1, width)


def solution(mesh):
    in_specs = (
        P(None, None, "energy", "rows", None),
        P(None, None, None, "rows", "energy"),
        P(None, "energy", "rows", None, None, None),
        P(),
        P("rows"),
    )
    out_specs = P(None, None, "energy", "rows", None)
    return jax.shard_map(shards, mesh=mesh, in_specs=in_specs, out_specs=out_specs, check_vma=False)
```

```python
import functools
import math

import jax
import jax.numpy as jnp
from jax import lax
from jax.experimental import pallas as pl
from jax.experimental.pallas import tpu as pltpu
from jax.sharding import PartitionSpec as P

F32 = jnp.float32
BF16 = jnp.bfloat16
VMEM = pl.BlockSpec(memory_space=pltpu.VMEM)
SMEM = pl.BlockSpec(memory_space=pltpu.SMEM)
HBM = pl.BlockSpec(memory_space=pltpu.HBM)


def call(kernel, out_shape, in_specs, flops, scratch=(), moved=2**20):
    return pl.pallas_call(
        kernel,
        out_shape=out_shape,
        in_specs=in_specs,
        out_specs=jax.tree.map(lambda _: VMEM, out_shape),
        scratch_shapes=list(scratch),
        compiler_params=pltpu.CompilerParams(vmem_limit_bytes=16 * 2**20),
        cost_estimate=pl.CostEstimate(flops=flops, bytes_accessed=moved, transcendentals=0),
    )


def exchange_order(count):
    middle = count // 2 + 1
    step = 3 if math.gcd(3, count) == 1 else 1
    return [(middle + step * at) % count for at in range(count)]


def split_high_low(values):
    high = values.astype(BF16)
    return high, (values - high.astype(F32)).astype(BF16)


def wrap(values, count):
    return values & (count - 1) if count & (count - 1) == 0 else values % count


def parts_of(values, count):
    return values >> (count.bit_length() - 1) if count & (count - 1) == 0 else values // count


def phases(energy, time, quarter, count):
    turns = wrap(4 * energy * time + count * quarter, 4 * count)
    half = jnp.where(turns >= 2 * count, turns - 2 * count, turns)
    odd = half >= count
    angle = jnp.where(odd, half - count, half).astype(F32) * (0.5 * math.pi / count)
    square = angle * angle
    cosine, sine = 0.0, 0.0
    for power in range(7, -1, -1):
        cosine = cosine * square + (-1) ** power / math.factorial(2 * power)
        sine = sine * square + (-1) ** power / math.factorial(2 * power + 1)
    value = jnp.where(odd, -sine * angle, cosine)
    return jnp.where(turns >= 2 * count, -value, value)


def table_plan(total, order):
    slots = total // len(order)
    size = 4 * total
    row = lax.broadcasted_iota(jnp.int32, (size, 1), 0)
    col = lax.broadcasted_iota(jnp.int32, (1, size), 1)

    def device_at(place):
        found = jnp.zeros_like(place)
        for at, device in enumerate(order):
            found = jnp.where(place == at, device, found)
        return found

    same = lax.broadcasted_iota(jnp.int32, (total, total), 0) == lax.broadcasted_iota(jnp.int32, (total, total), 1)
    source = device_at(parts_of(col, 4 * slots)) * slots + wrap(col, slots)
    first = (
        lax.broadcasted_iota(jnp.int32, (total, size), 0) == source,
        wrap(row, total),
        wrap(parts_of(row, total), 2) - wrap(parts_of(col, slots), 2),
        parts_of(row, 2 * total) == wrap(parts_of(col, 2 * slots), 2),
    )
    source = device_at(parts_of(row, 4 * slots)) * slots + wrap(parts_of(row, 4), slots)
    second = (
        lax.broadcasted_iota(jnp.int32, (size, total), 1) == source,
        wrap(col, total),
        1 - wrap(row, 2) + wrap(parts_of(col, total), 2),
        wrap(parts_of(row, 2), 2) == parts_of(col, 2 * total),
    )
    return same, first, second


def tables(energy_order, plan):
    total = energy_order.shape[1]
    same, first, second = plan
    down = jnp.sum(jnp.where(same, energy_order, 0), axis=1, keepdims=True)
    pick, time, quarter, keep = first
    energy = jnp.sum(jnp.where(pick, down, 0), axis=0, keepdims=True)
    there = jnp.where(keep, phases(energy, time, quarter, total), 0.0)
    pick, time, quarter, keep = second
    energy = jnp.sum(jnp.where(pick, energy_order, 0), axis=1, keepdims=True)
    back = jnp.where(keep, phases(energy, time, quarter, total), 0.0) * (1.0 / total)
    return there, back


def row_positions(slab, devices, shape):
    at = lax.broadcasted_iota(jnp.int32, shape, 0)
    return wrap(at, devices) * (slab // devices) + parts_of(at, devices)


def to_tiles(tiles_ref, values, start=0):
    rows, lanes = values.shape
    for tile in range(tiles_ref.shape[0]):
        last = min(lanes, 128 * (tile + 1))
        tiles_ref[tile, pl.ds(start, rows), : last - 128 * tile] = values[:, 128 * tile : last]


def strided_rows(tiles_ref, start, count, stride, lanes):
    found = [tiles_ref[tile, pl.ds(start, count, stride=stride), :] for tile in range(tiles_ref.shape[0])]
    return jnp.concatenate(found, axis=1)[:, :lanes]


def front_kernel(
    order,
    energy_hbm,
    green_hbm,
    out_ref,
    first_ref,
    second_ref,
    energy_ref,
    green_ref,
    sems,
):
    pairs, slots, entries = green_ref.shape
    copies = [pltpu.make_async_copy(energy_hbm, energy_ref, sems.at[pairs])]
    copies += [pltpu.make_async_copy(green_hbm.at[at], green_ref.at[at], sems.at[at]) for at in range(pairs)]
    for copy in copies:
        copy.start()
    plan = table_plan(energy_ref.shape[1], order)
    copies[0].wait()
    first, second = tables(energy_ref[...], plan)
    first_high, first_low = split_high_low(first)
    second_high, second_low = split_high_low(second)
    first_ref[...] = jnp.concatenate([first_high, first_low], axis=1)
    second_ref[...] = jnp.concatenate([second_high, second_low, second_high], axis=1)
    for copy in copies[1:]:
        copy.wait()
    columns = entries // len(order)
    whole = jnp.concatenate([green_ref[at].astype(F32) for at in range(pairs)], axis=0)
    parts = [whole[:, device * columns : (device + 1) * columns] for device in order]
    out_ref[...] = jnp.concatenate(parts, axis=0).astype(BF16)


def convolve_kernel(first_ref, second_ref, spread_ref, screen_ref, out_ref):
    total = screen_ref.shape[0] // 4
    spread = spread_ref[...]
    times = jnp.dot(first_ref[...], jnp.concatenate([spread, spread], axis=0), preferred_element_type=F32)
    screen = screen_ref[...].astype(F32)
    mixed = []
    for kind in range(2):
        base = kind * 2 * total
        times_re, times_im = times[base : base + total], times[base + total : base + 2 * total]
        screen_re, screen_im = screen[base : base + total], screen[base + total : base + 2 * total]
        mixed.append(times_re * screen_re - times_im * screen_im)
        mixed.append(times_re * screen_im + times_im * screen_re)
    mixed_high, mixed_low = split_high_low(jnp.concatenate(mixed, axis=0))
    sigma = jnp.dot(
        second_ref[...],
        jnp.concatenate([mixed_high, mixed_high, mixed_low], axis=0),
        preferred_element_type=F32,
    ).astype(BF16)
    out_ref[0] = sigma
    out_ref[1] = sigma


def spread_rows(sigma_ref, wide_ref, slab, padded, places):
    devices = len(places)
    each = sigma_ref.shape[0] // devices
    depth = slab // devices
    wide = sigma_ref[...].astype(F32)
    lanes = wide_ref.shape[0] * 128
    wide = jnp.concatenate([wide, jnp.zeros((wide.shape[0], lanes - wide.shape[1]), F32)], axis=1)
    for at, device in enumerate(places):
        to_tiles(wide_ref, wide[at * each : (at + 1) * each], device * each)
    matrices = []
    for at in range(each):
        flat = strided_rows(wide_ref, at, devices, each, lanes)
        matrices.append(
            jnp.concatenate([flat[:, slab * i : slab * i + padded] for i in range(depth)], axis=0)
        )
    return matrices


def row_order(slab, devices):
    shape = (slab, slab)
    return jnp.where(
        row_positions(slab, devices, shape) == lax.broadcasted_iota(jnp.int32, shape, 1), 1.0, 0.0
    ).astype(BF16)


def neighbour_density(matrices, blocks_ref, slot, block, ordering):
    real, imag = blocks_ref[0, slot, block], blocks_ref[1, slot, block]
    slab, width = real.shape
    gap = jnp.zeros((matrices[0].shape[1] - slab, width), BF16)
    left = jnp.concatenate(
        [
            jnp.concatenate([matrices[slot * 4 + kind * 2], matrices[slot * 4 + kind * 2 + 1]], axis=1)
            for kind in range(2)
        ],
        axis=0,
    ).astype(BF16)
    inner_re = jnp.dot(left, jnp.concatenate([real, gap, imag, gap], axis=0), preferred_element_type=F32)
    inner_im = jnp.dot(left, jnp.concatenate([-imag, gap, real, gap], axis=0), preferred_element_type=F32)
    wide_re = jnp.dot(ordering, real, preferred_element_type=F32)
    wide_im = jnp.dot(ordering, imag, preferred_element_type=F32)
    result = []
    for kind in range(2):
        z_re = inner_re[kind * slab : (kind + 1) * slab]
        z_im = inner_im[kind * slab : (kind + 1) * slab]
        result.append((z_re * wide_re - z_im * wide_im, z_re * wide_im + z_im * wide_re))
    return result


def density_kernel(order, rows, padded, start_ref, sigma_ref, blocks_ref, out_ref, wide_ref):
    slots, _, slab, width = blocks_ref.shape[1:]
    devices = len(order)
    row = lax.axis_index("rows")
    odd = lax.rem(row, 2)
    has_far = jnp.where(jnp.logical_and(row > 0, row < rows - 1), 1.0, 0.0)
    own = spread_rows(sigma_ref.at[1 - odd], wide_ref.at[0], slab, padded, order)
    far = spread_rows(sigma_ref.at[odd], wide_ref.at[1], slab, padded, order)
    on_diagonal = row_positions(slab, devices, (slab, padded)) == lax.broadcasted_iota(jnp.int32, (slab, padded), 1)
    diagonal = jnp.concatenate(
        [jnp.sum(jnp.where(on_diagonal, matrix, 0.0), axis=0, keepdims=True) for matrix in own], axis=0
    )
    at_row = lax.broadcasted_iota(jnp.int32, (padded, width), 0)
    placed = at_row + start_ref[0] == lax.broadcasted_iota(jnp.int32, (padded, width), 1)
    place = jnp.where(jnp.logical_and(placed, at_row < slab), 1.0, 0.0).astype(BF16)
    direct = jnp.dot(diagonal.astype(BF16), place, preferred_element_type=F32)
    ordering = row_order(slab, devices)
    for slot in range(slots):
        here = neighbour_density(own, blocks_ref, slot, 1, ordering)
        there = neighbour_density(far, blocks_ref, slot, 2 * odd, ordering)
        for kind in range(2):
            for part in range(2):
                at = slot * 4 + kind * 2 + part
                out_ref[(kind * 2 + part) * slots + slot] = direct[at : at + 1] + jnp.sum(
                    here[kind][part] + there[kind][part] * has_far, axis=0, keepdims=True
                )


def density_near_kernel(order, padded, sigma_ref, blocks_ref, before_ref, out_ref, wide_ref):
    slots, _, slab, _ = blocks_ref.shape[1:]
    near = spread_rows(sigma_ref, wide_ref, slab, padded, order)
    ordering = row_order(slab, len(order))
    block = 2 - 2 * lax.rem(lax.axis_index("rows"), 2)
    for slot in range(slots):
        found = neighbour_density(near, blocks_ref, slot, block, ordering)
        for kind in range(2):
            for part in range(2):
                at = (kind * 2 + part) * slots + slot
                out_ref[at] = before_ref[at] + jnp.sum(found[kind][part], axis=0, keepdims=True)


def shards(green_window, screened, retarded, energy_order, window_start):
    devices = lax.axis_size("energy")
    rows = lax.axis_size("rows")
    slots, entries = green_window.shape[2], green_window.shape[4]
    slab, width = retarded.shape[4], retarded.shape[5]
    total = devices * slots
    columns = entries // devices
    order = exchange_order(devices)
    padded = pl.cdiv(slab, 128) * 128

    def stay(values):
        return pltpu.with_memory_space_constraint(values, pltpu.HBM)

    packed, first, second = call(
        functools.partial(front_kernel, order),
        (
            jax.ShapeDtypeStruct((4 * total, columns), BF16),
            jax.ShapeDtypeStruct((4 * total, 2 * 4 * total), BF16),
            jax.ShapeDtypeStruct((4 * total, 3 * 4 * total), BF16),
        ),
        [HBM] * 2,
        1000,
        [
            pltpu.VMEM((1, total), jnp.int32),
            pltpu.VMEM((4, slots, entries), BF16),
            pltpu.SemaphoreType.DMA((5,)),
        ],
    )(stay(energy_order.reshape(1, total)), stay(green_window.reshape(4, slots, entries)))
    odd = lax.axis_index("rows") % 2 == 1
    packed, first, second, odd = lax.optimization_barrier((packed, first, second, odd))
    spread = lax.all_to_all(
        packed, "energy", split_axis=0, concat_axis=0, tiled=True, axis_index_groups=[order]
    )
    sigma = call(
        convolve_kernel,
        jax.ShapeDtypeStruct((2, 4 * total, columns), BF16),
        [VMEM] * 4,
        2 * 5 * 16 * total * total * columns,
    )(first, second, spread, screened.reshape(4 * total, columns))

    groups = [
        [energy * rows + (low + side) % rows for side in range(2) for energy in order]
        for low in range(1, rows, 2)
    ]
    both = lax.all_to_all(
        sigma.reshape(2 * devices, 4 * slots, columns),
        ("energy", "rows"),
        split_axis=0,
        concat_axis=0,
        tiled=True,
        axis_index_groups=groups,
    ).reshape(2, 4 * total, columns)
    own = jnp.where(odd, both[0], both[1])
    pairs = [(row, row ^ 1) for row in range(rows)]
    near = lax.ppermute(own, "rows", pairs)

    blocks = retarded.reshape(2, slots, 3, slab, width)
    wide = (pl.cdiv(columns + padded - slab, 128), 4 * total, 128)
    out = jax.ShapeDtypeStruct((4 * slots, 1, width), F32)
    work = 2 * 8 * slots * 2 * slab * slab * width
    density = call(
        functools.partial(density_kernel, order, rows, padded),
        out,
        [SMEM] + [VMEM] * 2,
        2 * work,
        [pltpu.VMEM((2, *wide), F32)],
    )(window_start, both, blocks)
    density = call(
        functools.partial(density_near_kernel, order, padded),
        out,
        [VMEM] * 3,
        work,
        [pltpu.VMEM(wide, F32)],
    )(near, blocks, density)
    return density.reshape(2, 2, slots, 1, width)


def solution(mesh):
    in_specs = (
        P(None, None, "energy", "rows", None),
        P(None, None, None, "rows", "energy"),
        P(None, "energy", "rows", None, None, None),
        P(),
        P("rows"),
    )
    out_specs = P(None, None, "energy", "rows", None)
    return jax.shard_map(shards, mesh=mesh, in_specs=in_specs, out_specs=out_specs, check_vma=False)
```
